256 devices in a mesh: section: 2 (over y_lo), dp: 4 (over y_hi, core), vocab: 32 (over z, x).
Axes of the slice: x: 4, y: 4 (y_hi: 2, y_lo: 2; y = y_hi * 2 + y_lo), z: 8, core: 2. Of those that a mesh axis runs over, the one named last changes fastest.
Arguments:
- stacked_rows: bfloat16 [2, 384, 4608], P('section', ('dp', 'vocab')), as said below
- tied_table: bfloat16 [131072, 4608], P(('section', 'dp', 'vocab')), as said below
- row_ids: int32 [2, 384], replicated, may hold values from 0 to 131071, as said below
Outputs:
- table_grad: bfloat16 [131072, 4608], P(('section', 'dp', 'vocab'))
- hidden_grad: bfloat16 [384, 4608], P(('dp', 'vocab'))
The draws below stay inside these ranges and needn't reach their ends.
Inputs may be any that keep to these rules, and one draw needn't show every extreme that they name: `stacked_rows`: rows of slot 0 and slot 1 are real-valued draws. `tied_table`: Real-valued table rows. `row_ids`: token ids of the vocabulary; an id may recur.
All inputs are finite; a program needn't handle non-finite values.
Results may differ from the reference program's by a relative error of at most 0.007.
Values may be sent and summed in bfloat16 or wider, within the bound.
No kernel may reach another device: no remote copies, remote signals or barrier semaphores. Data moves between devices by JAX's collectives and lax.ppermute only.
A program may use at most 128 MiB of HBM per device.

```python
import math
import jax
import jax.numpy as jnp
from jax import lax

D = 4608
VOCAB = 131072
DPROWS = 384


quiet_scale = 0.02


key_scale = 1.5


def shared_ids(key):
    limits = jax.random.randint(jax.random.fold_in(key, 200), (2, DPROWS), 1, VOCAB + 1)
    raw_ids = jax.random.randint(jax.random.fold_in(key, 201), (2, DPROWS), 0, VOCAB)
    shuffled = jax.random.permutation(jax.random.fold_in(key, 202), VOCAB)
    token_ids = shuffled[raw_ids % limits]
    places = jax.random.randint(jax.random.fold_in(key, 203), (2,), 0, DPROWS)
    second_place = (places[0] + 1 + places[1] % (DPROWS - 1)) % DPROWS
    token_ids = token_ids.at[0, places[0]].set(VOCAB - 1)
    token_ids = token_ids.at[0, second_place].set(0)
    chosen = jax.random.permutation(jax.random.fold_in(key, 204), VOCAB)[:2 * DPROWS]
    return (token_ids.astype(jnp.int32), chosen.astype(jnp.int32))


def shared_table(key, low_log, high_log):
    token_ids, chosen = shared_ids(key)
    base = jax.random.normal(key, (VOCAB, D), jnp.float32)
    spread = jnp.exp(jax.random.uniform(jax.random.fold_in(key, 100), (VOCAB,), jnp.float32, low_log, high_log))
    place = jnp.arange(VOCAB, dtype=jnp.float32) / VOCAB
    scales = 2.0 * jnp.exp(place * math.log(1.3)) * spread
    targeted = jnp.zeros((VOCAB,), jnp.float32).at[token_ids[1]].set(1.0)
    pooled = jnp.zeros((VOCAB,), jnp.float32).at[chosen].set(1.0)
    scales = jnp.where(targeted > 0.5, quiet_scale * scales, scales)
    scales = jnp.where(pooled > 0.5, key_scale, scales)
    return (base, scales)


def draw_row_ids(key, part):
    token_ids, chosen = shared_ids(key)
    return token_ids


def draw_tied_table(key, part):
    low_log, high_log = (math.log(0.8), math.log(1.25))
    base, scales = shared_table(key, low_log, high_log)
    return (base * scales[:, None] / math.sqrt(D)).astype(jnp.bfloat16)


def draw_stacked_rows(key, part):
    key = jax.random.fold_in(key, 2)
    noise = jax.random.normal(key, (2, DPROWS, D), jnp.float32)
    first = 0.05 * noise[0]
    second = noise[1]
    return jnp.stack([first, second]).astype(jnp.bfloat16)


def setup_inputs(seed: int = 0) -> dict:
    key_of = jax.random.split(jax.random.key(seed), 4)
    stacked_rows = draw_stacked_rows(jax.random.fold_in(key_of[3], 71), 0)
    tied_table = draw_tied_table(jax.random.fold_in(key_of[3], 71), 0)
    row_ids = draw_row_ids(jax.random.fold_in(key_of[3], 71), 0)
    return dict(stacked_rows=stacked_rows, tied_table=tied_table, row_ids=row_ids)


def reference(stacked_rows, tied_table, row_ids):
    cotangent = stacked_rows[0]
    hidden = stacked_rows[1]
    factor = jnp.asarray(math.sqrt(D), jnp.float32).astype(jnp.bfloat16).astype(jnp.float32)
    columns = jnp.arange(VOCAB, dtype=jnp.int32)
    onehot = (row_ids[1][:, None] == columns[None, :]).astype(jnp.float32)
    logits = jnp.dot(hidden, tied_table.T, preferred_element_type=jnp.float32)
    highest = lax.optimization_barrier(jnp.max(logits, axis=1, keepdims=True))
    expvals = jnp.exp(logits - highest)
    probability = expvals / lax.optimization_barrier(jnp.sum(expvals, axis=1, keepdims=True))
    coefficient = (probability - onehot).astype(jnp.bfloat16)
    embed_grad = factor * jax.ops.segment_sum(cotangent.astype(jnp.float32), row_ids[0], VOCAB)
    head_grad = jnp.dot(coefficient.T, hidden, preferred_element_type=jnp.float32)
    table_grad = (head_grad + embed_grad).astype(jnp.bfloat16)
    hidden_grad = jnp.dot(coefficient, tied_table, preferred_element_type=jnp.float32).astype(jnp.bfloat16)
    return (table_grad, hidden_grad)
```

```python
import math

import jax
import jax.numpy as jnp
from jax import lax
from jax.sharding import PartitionSpec as P

D = 4608
HALF = D // 2
AXES = ("section", "dp", "vocab")
SIZES = {"yl": 2, "yh": 2, "core": 2, "z": 8, "x": 4}


def place(device):
    vocab, dp, section = device % 32, device // 32 % 4, device // 128
    return {"yl": section, "yh": dp // 2, "core": dp % 2, "z": vocab // 4, "x": vocab % 4}


def groups(*axes):
    found = {}
    for device in range(256):
        at = place(device)
        key = tuple(at[a] for a in SIZES if a not in axes)
        found.setdefault(key, []).append((tuple(at[a] for a in axes), device))
    return [[device for _, device in sorted(members)] for members in found.values()]


def exchange(blocks, *axes):
    return lax.all_to_all(blocks, AXES, 0, 0, axis_index_groups=groups(*axes), tiled=True)


def other_core(array):
    pairs = [pair for a, b in groups("core") for pair in ((a, b), (b, a))]
    return lax.ppermute(array, AXES, pairs)


def by_core(ids):
    return ids.reshape(2, 2, 8, 4, 3).transpose(1, 0, 3, 2, 4).reshape(2, 192)


def shards(stacked_rows, tied_table, row_ids):
    factor = jnp.asarray(math.sqrt(D), jnp.float32).astype(jnp.bfloat16)
    shard_rows = tied_table.shape[0]
    core = lax.axis_index("dp") % 2
    owner = (lax.axis_index("section") * 4 + lax.axis_index("dp")) * 32 + lax.axis_index("vocab")
    columns = owner * shard_rows + lax.iota(jnp.int32, shard_rows)
    table = (tied_table[:, :HALF], tied_table[:, HALF:])

    with jax.named_scope("rows_lz"):
        own = stacked_rows[0].reshape(3, 2, HALF).transpose(1, 0, 2)
        blocks = jnp.broadcast_to(own[:, None], (2, 8, 3, HALF)).reshape(16, 3, HALF)
        got = exchange(blocks, "yl", "z").reshape(2, 24, HALF)
    with jax.named_scope("cotangent"):
        cotangent = lax.all_gather(
            got[0], AXES, axis_index_groups=groups("yl", "core", "yh", "x"), axis=0, tiled=True
        ).reshape(2, 384, HALF)
    with jax.named_scope("hidden_xy"):
        mine = exchange(jnp.broadcast_to(got[1], (16, 24, HALF)), "yl", "yh", "x").reshape(2, 192, HALF)
    with jax.named_scope("hidden_core"):
        hidden = jnp.concatenate([mine, other_core(mine)], axis=1)

    with jax.named_scope("logits"):
        logits = sum(
            lax.dot_general(hidden[i], table[i], (((1,), (1,)), ((), ())), preferred_element_type=jnp.float32)
            for i in range(2)
        )
    with jax.named_scope("stats"):
        high = jnp.max(logits, axis=1)
        total = jnp.sum(jnp.exp(logits - high[:, None]), axis=1)
        stats = jnp.stack([high, total]).reshape(2, 2, 192)
        stats = jnp.where(core == 0, stats, stats[:, ::-1]).reshape(1, 2, 384)

        def combine(parts):
            top = jnp.max(parts[:, 0], axis=0)
            return jnp.stack([top, jnp.sum(parts[:, 1] * jnp.exp(parts[:, 0] - top), axis=0)])[None]

        stats = combine(exchange(jnp.broadcast_to(stats, (32, 2, 384)), "yl", "yh", "x", "core"))
        stats = combine(exchange(jnp.broadcast_to(stats, (8, 2, 384)), "z"))
        stats = stats.reshape(2, 2, 192)
        stats = jnp.where(core == 0, stats, stats[:, ::-1]).reshape(2, 384)

    with jax.named_scope("coefficient"):
        targets = by_core(row_ids[1])
        targets = jnp.where(core == 0, targets, targets[::-1]).reshape(384)
        onehot = (targets[:, None] == columns[None, :]).astype(jnp.float32)
        coefficient = (jnp.exp(logits - stats[0][:, None]) / stats[1][:, None] - onehot).astype(jnp.bfloat16)

    with jax.named_scope("hidden_grad"):
        partial = jnp.stack(
            [jnp.dot(coefficient, table[i], preferred_element_type=jnp.float32) for i in range(2)]
        )
        theirs = other_core(partial[:, 192:].astype(jnp.bfloat16))
        chip = (partial[:, :192] + theirs.astype(jnp.float32)).astype(jnp.bfloat16)
        plane = exchange(chip.reshape(16, 24, HALF), "yl", "yh", "x")
        plane = jnp.sum(plane.astype(jnp.float32), axis=0).astype(jnp.bfloat16).reshape(1, 8, 3, HALF)
        last = exchange(jnp.broadcast_to(plane, (2, 8, 3, HALF)).reshape(16, 3, HALF), "yl", "z")
        last = jnp.sum(last.reshape(2, 8, 3, HALF).astype(jnp.float32), axis=1)
        hidden_grad = last.transpose(1, 0, 2).reshape(3, D).astype(jnp.bfloat16)

    with jax.named_scope("table_grad"):
        inputs = by_core(row_ids[0]).reshape(384)
        placed = jnp.where(inputs[:, None] == columns[None, :], factor, jnp.zeros((), jnp.bfloat16))
        left = jnp.concatenate([coefficient, placed], axis=0)
        right = jnp.concatenate([hidden, cotangent], axis=1)
        table_grad = jnp.concatenate(
            [
                lax.dot_general(left, right[i], (((0,), (0,)), ((), ())), preferred_element_type=jnp.float32)
                for i in range(2)
            ],
            axis=1,
        ).astype(jnp.bfloat16)
    return (table_grad, hidden_grad)


def solution(mesh):
    placed = (P("section", ("dp", "vocab"), None), P(("section", "dp", "vocab"), None), P())
    return jax.shard_map(
        shards,
        mesh=mesh,
        in_specs=placed,
        out_specs=(P(("section", "dp", "vocab"), None), P(("dp", "vocab"), None)),
        check_vma=False,
    )
```

```python
import math

import jax
import jax.numpy as jnp
from jax import lax
from jax.experimental import pallas as pl
from jax.experimental.pallas import tpu as pltpu
from jax.sharding import PartitionSpec as P

D = 4608
HALF = D // 2
ROWS = 384
CORE_ROWS = 192
CHUNK = 768
PER_HALF = HALF // CHUNK
AXES = ("section", "dp", "vocab")
SIZES = {"yl": 2, "yh": 2, "core": 2, "z": 8, "x": 4}
FACTOR = float(jnp.bfloat16(math.sqrt(D)))


def place(device):
    vocab, dp, section = device % 32, device // 32 % 4, device // 128
    return {"yl": section, "yh": dp // 2, "core": dp % 2, "z": vocab // 4, "x": vocab % 4}


def device_at(at):
    return (at["yl"] * 4 + at["yh"] * 2 + at["core"]) * 32 + at["z"] * 4 + at["x"]


def groups(*axes):
    found = {}
    for device in range(256):
        at = place(device)
        key = tuple(at[a] for a in SIZES if a not in axes)
        found.setdefault(key, []).append((tuple(at[a] for a in axes), device))
    return [[device for _, device in sorted(members)] for members in found.values()]


def exchange(blocks, *axes):
    return lax.all_to_all(blocks, AXES, 0, 0, axis_index_groups=groups(*axes), tiled=True)


def other_core(array):
    pairs = [pair for a, b in groups("core") for pair in ((a, b), (b, a))]
    return lax.ppermute(array, AXES, pairs)


def from_x(array, offset):
    pairs = []
    for device in range(256):
        at = place(device)
        pairs.append((device_at(dict(at, x=(at["x"] + offset) % 4)), device))
    return lax.ppermute(array, AXES, pairs)


def from_y(array, offset):
    pairs = []
    for device in range(256):
        at = place(device)
        y = (at["yh"] * 2 + at["yl"] + offset) % 4
        pairs.append((device_at(dict(at, yh=y // 2, yl=y % 2)), device))
    return lax.ppermute(array, AXES, pairs)


def natural_row(yh, core, z, x, j):
    return ((yh * 2 + core) * 32 + z * 4 + x) * 3 + j


def params(**more):
    return pltpu.CompilerParams(vmem_limit_bytes=14 * 2**20, **more)


def pick(condition, a, b):
    return jnp.where(condition, a, b)


def hold_kernel(source, held, arrived):
    copy = pltpu.make_async_copy(source, held, arrived)
    copy.start()
    copy.wait()


def hold(array):
    return pl.pallas_call(
        hold_kernel,
        in_specs=[pl.BlockSpec(memory_space=pltpu.MemorySpace.HBM)],
        out_specs=pl.BlockSpec(memory_space=pltpu.VMEM),
        out_shape=pltpu.VMEM(array.shape, array.dtype),
        scratch_shapes=[pltpu.SemaphoreType.DMA],
        compiler_params=params(),
        name="hold",
    )(array)


def ids_onehot(ids, first, order, value):
    column = first + lax.broadcasted_iota(jnp.int32, (512, ROWS), 0)
    plain = jnp.where(column == ids, jnp.float32(value), jnp.float32(0)).astype(jnp.bfloat16)
    natural = lax.broadcasted_iota(jnp.int32, (ROWS, order.shape[1]), 0)
    move = jnp.where(natural == order, jnp.float32(1), jnp.float32(0)).astype(jnp.bfloat16)
    return jnp.dot(plain, move, preferred_element_type=jnp.float32)


SCALARS = pl.BlockSpec(memory_space=pltpu.SMEM)
BLOCK = pl.BlockSpec(memory_space=pltpu.VMEM)


def stats_kernel(at, mine, other, out):
    rows = []
    for logits in (mine, other):
        turned = logits[...].T
        high = jnp.max(turned, axis=0, keepdims=True)
        rows.append((high, jnp.sum(jnp.exp(turned - high), axis=0, keepdims=True)))
    first = at[0] == 0
    both = [pick(first, rows[i][k], rows[1 - i][k]) for k in range(2) for i in range(2)]
    out[...] = jnp.broadcast_to(jnp.concatenate(both, axis=0)[None], out.shape)


def merged(parts):
    high = jnp.max(parts[:, 0:2, :], axis=0)
    total = jnp.sum(parts[:, 2:4, :] * jnp.exp(parts[:, 0:2, :] - high), axis=0)
    return high, total


def merge_kernel(parts, out):
    out[...] = jnp.broadcast_to(jnp.concatenate(merged(parts[...]), axis=0)[None], out.shape)


def coefficient_kernel(at, mine, other, parts, ids, orders, out_mine, out_other, turned_mine, turned_other):
    high, total = merged(parts[...])
    scale = 1.0 / total
    first = at[0] == 0
    for i, (logits, out, turned) in enumerate(((mine, out_mine, turned_mine), (other, out_other, turned_other))):
        top = pick(first, high[i : i + 1], high[1 - i : 2 - i])
        factor = pick(first, scale[i : i + 1], scale[1 - i : 2 - i])
        onehot = ids_onehot(ids[1:2, :], at[2], orders[i : i + 1, :], 1.0)
        values = jnp.exp(logits[...].T - top) * factor - onehot
        turned[...] = values.astype(jnp.bfloat16)
        out[...] = values.T.astype(jnp.bfloat16)


def small_call(kernel, name, outs, *args):
    return pl.pallas_call(
        kernel,
        in_specs=[SCALARS if a.ndim == 1 else BLOCK for a in args],
        out_specs=[BLOCK] * len(outs),
        out_shape=[jax.ShapeDtypeStruct(*out) for out in outs],
        compiler_params=params(),
        name=name,
    )(*args)


def table_grad_kernel(at, coef_mine, coef_other, ids, orders, mine, other, a0, a1, a2, a3, b0, b1, b2, b3, out, placed):
    part, step = pl.program_id(0), pl.program_id(1)

    @pl.when(step == 0)
    def _():
        order = jnp.where(part == 0, orders[0:1, :], orders[1:2, :])
        placed[...] = ids_onehot(ids[0:1, :], at[2], order, FACTOR).astype(jnp.bfloat16)

    even = part == 0
    cotangent = jnp.concatenate(
        [
            pick(even, a0[...], a1[...]),
            pick(even, a2[...], a3[...]),
            pick(even, b0[...], b1[...]),
            pick(even, b2[...], b3[...]),
        ],
        axis=0,
    )
    total = jnp.dot(placed[...], cotangent, preferred_element_type=jnp.float32)
    total += jnp.dot(coef_mine[...], mine[0], preferred_element_type=jnp.float32)
    total += jnp.dot(coef_other[...], other[0], preferred_element_type=jnp.float32)
    out[...] = total.astype(jnp.bfloat16)


def table_grad_call(at, coef_mine, coef_other, ids, orders, mine, other, own, far):
    whole = lambda *shape: pl.BlockSpec(shape, lambda p, k, at: (0,) * len(shape))
    side = lambda p, at: lax.bitwise_xor(at[1], p)
    block = pl.BlockSpec((1, CORE_ROWS, CHUNK), lambda p, k, at: (side(p, at), 0, k))
    early = pl.BlockSpec((96, CHUNK), lambda p, k, at: (0, k * (1 - p) + (PER_HALF - 1) * p))
    late = pl.BlockSpec((96, CHUNK), lambda p, k, at: (0, k * p))
    return pl.pallas_call(
        table_grad_kernel,
        grid_spec=pltpu.PrefetchScalarGridSpec(
            num_scalar_prefetch=1,
            grid=(2, PER_HALF),
            in_specs=[whole(512, CORE_ROWS)] * 2 + [whole(2, ROWS), whole(2, ROWS), block, block]
            + [early, late, early, late] * 2,
            out_specs=pl.BlockSpec((512, CHUNK), lambda p, k, at: (0, side(p, at) * PER_HALF + k)),
            scratch_shapes=[pltpu.VMEM((512, ROWS), jnp.bfloat16)],
        ),
        out_shape=jax.ShapeDtypeStruct((512, D), jnp.bfloat16),
        compiler_params=params(),
        cost_estimate=pl.CostEstimate(flops=4 * ROWS * 512 * D, bytes_accessed=13_000_000, transcendentals=0),
        name="table_grad",
    )(at, coef_mine, coef_other, ids, orders, mine, other, *own, *far)


def shards(stacked_rows, tied_table, row_ids):
    section, dp, vocab = (lax.axis_index(a) for a in AXES)
    core, yh, x = dp % 2, dp // 2, vocab % 4
    first_column = ((section * 4 + dp) * 32 + vocab) * tied_table.shape[0]
    at = jnp.stack([core, section, first_column]).astype(jnp.int32)

    with jax.named_scope("orders"):
        i = lax.iota(jnp.int32, ROWS)
        c, yy, xx, z, j = i // 192, i // 96 % 2, i // 24 % 4, i // 3 % 8, i % 3
        moved_x = (x + xx) % 4
        y_of = lambda part: (yh * 2 + section + 2 * yy + part) % 4
        head_orders = natural_row(yy, lax.bitwise_xor(core, c), z, xx, j).reshape(2, CORE_ROWS)
        input_orders = jnp.stack(
            [natural_row(y_of(part) // 2, lax.bitwise_xor(core, c), z, moved_x, j) for part in range(2)]
        )

    with jax.named_scope("rows_lz"):
        own = stacked_rows[0].reshape(3, 2, HALF).transpose(1, 0, 2)
        blocks = jnp.broadcast_to(own[:, None], (2, 8, 3, HALF)).reshape(16, 3, HALF)
        got = exchange(blocks, "yl", "z").reshape(2, 24, HALF)
    with jax.named_scope("cotangent_x"):
        line = [got[0]] + [from_x(got[0], offset) for offset in (1, 2, 3)]
    with jax.named_scope("hidden_xy"):
        mine = exchange(jnp.broadcast_to(got[1], (16, 24, HALF)), "yl", "yh", "x").reshape(2, CORE_ROWS, HALF)
        line = jnp.concatenate(line, axis=0)
        mine, line, table, at, head_orders, input_orders = lax.optimization_barrier(
            (mine, line, tied_table, at, head_orders, input_orders)
        )
        table = hold(table)
    with jax.named_scope("hidden_core"):
        other = other_core(mine)
    with jax.named_scope("cotangent_y"):
        own = [line] + [from_y(line, offset) for offset in (1, 2, 3)]
    with jax.named_scope("logits"):
        logits = [
            sum(
                lax.dot_general(
                    rows[i], half, (((1,), (1,)), ((), ())), preferred_element_type=jnp.float32
                )
                for i, half in enumerate((table[:, :HALF], table[:, HALF:]))
            )
            for rows in (mine, other)
        ]
    with jax.named_scope("stats"):
        (stats,) = small_call(stats_kernel, "stats", [((32, 4, CORE_ROWS), jnp.float32)], at, *logits)
        stats = exchange(stats, "yl", "yh", "x", "core")
        (stats,) = small_call(merge_kernel, "merge", [((8, 4, CORE_ROWS), jnp.float32)], stats)
        stats = exchange(stats, "z")
    with jax.named_scope("coefficient"):
        *coefficient, turned_mine, turned_other = small_call(
            coefficient_kernel,
            "coefficient",
            [((CORE_ROWS, 512), jnp.bfloat16)] * 2 + [((512, CORE_ROWS), jnp.bfloat16)] * 2,
            at,
            *logits,
            stats,
            row_ids,
            head_orders,
        )
        *coefficient, own = lax.optimization_barrier((*coefficient, own))
    with jax.named_scope("hidden_grad"):
        halves = (table[:, :HALF], table[:, HALF:])
        product = lambda rows, half: jnp.dot(rows, half, preferred_element_type=jnp.float32)
        theirs = [other_core(product(coefficient[1], half).astype(jnp.bfloat16)) for half in halves]
        ours = lax.optimization_barrier([product(coefficient[0], half) for half in halves])
        chip = jnp.stack([(a + b).astype(jnp.bfloat16) for a, b in zip(ours, theirs)])
        chip, turned_mine, turned_other = lax.optimization_barrier((chip, turned_mine, turned_other))
    with jax.named_scope("table_grad"):
        far = [other_core(piece) for piece in own]
        table_grad = table_grad_call(at, turned_mine, turned_other, row_ids, input_orders, mine, other, own, far)
    with jax.named_scope("hidden_grad"):
        plane = exchange(chip.reshape(16, 24, HALF), "yl", "yh", "x")
        plane, table_grad = lax.optimization_barrier((plane, table_grad))
        plane = jnp.sum(plane.astype(jnp.float32), axis=0).astype(jnp.bfloat16).reshape(1, 8, 3, HALF)
        last = exchange(jnp.broadcast_to(plane, (2, 8, 3, HALF)).reshape(16, 3, HALF), "yl", "z")
        last = jnp.sum(last.reshape(2, 8, 3, HALF).astype(jnp.float32), axis=1)
        hidden_grad = last.transpose(1, 0, 2).reshape(3, D).astype(jnp.bfloat16)
    return (table_grad, hidden_grad)


def solution(mesh):
    placed = (P("section", ("dp", "vocab"), None), P(("section", "dp", "vocab"), None), P())
    return jax.shard_map(
        shards,
        mesh=mesh,
        in_specs=placed,
        out_specs=(P(("section", "dp", "vocab"), None), P(("dp", "vocab"), None)),
        check_vma=False,
    )
```

```python
import math

import jax
import jax.numpy as jnp
from jax import lax
from jax.experimental import pallas as pl
from jax.experimental.pallas import tpu as pltpu
from jax.sharding import PartitionSpec as P

D = 4608
HALF = D // 2
ROWS = 384
CORE_ROWS = 192
CHUNK = 1152
PER_HALF = HALF // CHUNK
AXES = ("section", "dp", "vocab")
SIZES = {"yl": 2, "yh": 2, "core": 2, "z": 8, "x": 4}
FACTOR = float(jnp.bfloat16(math.sqrt(D)))


def place(device):
    vocab, dp, section = device % 32, device // 32 % 4, device // 128
    return {"yl": section, "yh": dp // 2, "core": dp % 2, "z": vocab // 4, "x": vocab % 4}


def device_at(at):
    return (at["yl"] * 4 + at["yh"] * 2 + at["core"]) * 32 + at["z"] * 4 + at["x"]


def groups(*axes):
    found = {}
    for device in range(256):
        at = place(device)
        key = tuple(at[a] for a in SIZES if a not in axes)
        found.setdefault(key, []).append((tuple(at[a] for a in axes), device))
    return [[device for _, device in sorted(members)] for members in found.values()]


def exchange(blocks, *axes):
    return lax.all_to_all(blocks, AXES, 0, 0, axis_index_groups=groups(*axes), tiled=True)


def other_core(array):
    pairs = [pair for a, b in groups("core") for pair in ((a, b), (b, a))]
    return lax.ppermute(array, AXES, pairs)


def from_x(array, offset):
    pairs = []
    for device in range(256):
        at = place(device)
        pairs.append((device_at(dict(at, x=(at["x"] + offset) % 4)), device))
    return lax.ppermute(array, AXES, pairs)


def from_y(array, offset):
    pairs = []
    for device in range(256):
        at = place(device)
        y = (at["yh"] * 2 + at["yl"] + offset) % 4
        pairs.append((device_at(dict(at, yh=y // 2, yl=y % 2)), device))
    return lax.ppermute(array, AXES, pairs)


def natural_row(yh, core, z, x, j):
    return ((yh * 2 + core) * 32 + z * 4 + x) * 3 + j


def params(**more):
    return pltpu.CompilerParams(vmem_limit_bytes=14 * 2**20, **more)


def pick(condition, a, b):
    return jnp.where(condition, a, b)


def in_hbm(array):
    return pltpu.with_memory_space_constraint(array, pltpu.MemorySpace.HBM)


def hold_kernel(source, held, arrived):
    copy = pltpu.make_async_copy(source, held, arrived)
    copy.start()
    copy.wait()


def hold(array):
    return pl.pallas_call(
        hold_kernel,
        in_specs=[pl.BlockSpec(memory_space=pltpu.MemorySpace.HBM)],
        out_specs=pl.BlockSpec(memory_space=pltpu.VMEM),
        out_shape=pltpu.VMEM(array.shape, array.dtype),
        scratch_shapes=[pltpu.SemaphoreType.DMA],
        compiler_params=params(),
        name="hold",
    )(in_hbm(array))


def ids_onehot(ids, first, order, value):
    column = first + lax.broadcasted_iota(jnp.int32, (512, ROWS), 0)
    plain = jnp.where(column == ids, jnp.float32(value), jnp.float32(0)).astype(jnp.bfloat16)
    natural = lax.broadcasted_iota(jnp.int32, (ROWS, order.shape[1]), 0)
    move = jnp.where(natural == order, jnp.float32(1), jnp.float32(0)).astype(jnp.bfloat16)
    return jnp.dot(plain, move, preferred_element_type=jnp.float32)


HBM = pltpu.MemorySpace.HBM
SCALARS = pl.BlockSpec(memory_space=pltpu.SMEM)
BLOCK = pl.BlockSpec(memory_space=pltpu.VMEM)


def stats_kernel(at, mine, other, out):
    rows = []
    for logits in (mine, other):
        turned = logits[...].T
        high = jnp.max(turned, axis=0, keepdims=True)
        rows.append((high, jnp.sum(jnp.exp(turned - high), axis=0, keepdims=True)))
    first = at[0] == 0
    both = [pick(first, rows[i][k], rows[1 - i][k]) for k in range(2) for i in range(2)]
    out[...] = jnp.broadcast_to(jnp.concatenate(both, axis=0)[None], out.shape)


def merged(parts):
    high = jnp.max(parts[:, 0:2, :], axis=0)
    total = jnp.sum(parts[:, 2:4, :] * jnp.exp(parts[:, 0:2, :] - high), axis=0)
    return high, total


def merge_kernel(parts, out):
    out[...] = jnp.broadcast_to(jnp.concatenate(merged(parts[...]), axis=0)[None], out.shape)


def coefficient_kernel(at, mine, other, parts, head_mine, head_other, out_mine, out_other, turned_mine, turned_other, kept, sent):
    high, total = merged(parts[...])
    scale = 1.0 / total
    first = at[0] == 0
    copies = []
    sides = ((mine, head_mine, out_mine, turned_mine), (other, head_other, out_other, turned_other))
    for i, (logits, onehot, out, turned) in enumerate(sides):
        top = pick(first, high[i : i + 1], high[1 - i : 2 - i])
        factor = pick(first, scale[i : i + 1], scale[1 - i : 2 - i])
        values = jnp.exp(logits[...].T - top) * factor - onehot[...].astype(jnp.float32)
        kept[i] = values.astype(jnp.bfloat16)
        copy = pltpu.make_async_copy(kept.at[i], turned, sent.at[i])
        copy.start()
        copies.append(copy)
        out[...] = values.T.astype(jnp.bfloat16)
    for copy in copies:
        copy.wait()


def onehots_kernel(at, ids, head_orders, input_orders, head_mine, head_other, placed):
    for i, out in enumerate((head_mine, head_other)):
        out[...] = ids_onehot(ids[1:2, :], at[2], head_orders[i : i + 1, :], 1.0).astype(jnp.bfloat16)
    for i in range(2):
        placed[i] = ids_onehot(ids[0:1, :], at[2], input_orders[i : i + 1, :], FACTOR).astype(jnp.bfloat16)


def plane_kernel(blocks, out):
    total = blocks[0].astype(jnp.float32)
    for i in range(1, blocks.shape[0]):
        total += blocks[i].astype(jnp.float32)
    for k in range(8):
        rows = total[3 * k : 3 * k + 3].astype(jnp.bfloat16)
        out[k] = rows
        out[8 + k] = rows


def small_call(kernel, name, outs, *args, far_outs=(), scratch=()):
    return pl.pallas_call(
        kernel,
        in_specs=[SCALARS if a.ndim == 1 else BLOCK for a in args],
        out_specs=[BLOCK] * len(outs) + [pl.BlockSpec(memory_space=HBM)] * len(far_outs),
        out_shape=[jax.ShapeDtypeStruct(*out) for out in outs] + [HBM(*out) for out in far_outs],
        scratch_shapes=scratch,
        compiler_params=params(),
        name=name,
    )(*args)


def table_grad_kernel(at, coef_mine, coef_other, placed, mine, other, a0, a1, a2, a3, b0, b1, b2, b3, out):
    even = pl.program_id(0) == 0
    cotangent = jnp.concatenate(
        [
            pick(even, a0[...], a1[...]),
            pick(even, a2[...], a3[...]),
            pick(even, b0[...], b1[...]),
            pick(even, b2[...], b3[...]),
        ],
        axis=0,
    )
    total = jnp.dot(placed[0], cotangent, preferred_element_type=jnp.float32)
    total += jnp.dot(coef_mine[...], mine[0], preferred_element_type=jnp.float32)
    total += jnp.dot(coef_other[...], other[0], preferred_element_type=jnp.float32)
    out[...] = total.astype(jnp.bfloat16)


def table_grad_call(at, coef_mine, coef_other, placed, mine, other, own, far):
    whole = lambda *shape: pl.BlockSpec(shape, lambda p, k, at: (0,) * len(shape))
    side = lambda p, at: lax.bitwise_xor(at[1], p)
    block = pl.BlockSpec((1, CORE_ROWS, CHUNK), lambda p, k, at: (side(p, at), 0, k))
    early = pl.BlockSpec((96, CHUNK), lambda p, k, at: (0, k * (1 - p) + (PER_HALF - 1) * p))
    late = pl.BlockSpec((96, CHUNK), lambda p, k, at: (0, k * p))
    return pl.pallas_call(
        table_grad_kernel,
        grid_spec=pltpu.PrefetchScalarGridSpec(
            num_scalar_prefetch=1,
            grid=(2, PER_HALF),
            in_specs=[whole(512, CORE_ROWS)] * 2
            + [pl.BlockSpec((1, 512, ROWS), lambda p, k, at: (p, 0, 0)), block, block]
            + [early, late, early, late] * 2,
            out_specs=pl.BlockSpec((512, CHUNK), lambda p, k, at: (0, side(p, at) * PER_HALF + k)),
        ),
        out_shape=jax.ShapeDtypeStruct((512, D), jnp.bfloat16),
        compiler_params=params(),
        cost_estimate=pl.CostEstimate(flops=4 * ROWS * 512 * D, bytes_accessed=13_000_000, transcendentals=0),
        name="table_grad",
    )(at, *(in_hbm(a) for a in (coef_mine, coef_other, placed, mine, other, *own, *far)))


def shards(stacked_rows, tied_table, row_ids):
    section, dp, vocab = (lax.axis_index(a) for a in AXES)
    core, yh, x = dp % 2, dp // 2, vocab % 4
    first_column = ((section * 4 + dp) * 32 + vocab) * tied_table.shape[0]
    at = jnp.stack([core, section, first_column]).astype(jnp.int32)

    with jax.named_scope("orders"):
        i = lax.iota(jnp.int32, ROWS)
        c, yy, xx, z, j = i // 192, i // 96 % 2, i // 24 % 4, i // 3 % 8, i % 3
        moved_x = (x + xx) % 4
        y_of = lambda part: (yh * 2 + section + 2 * yy + part) % 4
        head_orders = natural_row(yy, lax.bitwise_xor(core, c), z, xx, j).reshape(2, CORE_ROWS)
        input_orders = jnp.stack(
            [natural_row(y_of(part) // 2, lax.bitwise_xor(core, c), z, moved_x, j) for part in range(2)]
        )

    with jax.named_scope("rows_lz"):
        own = stacked_rows[0].reshape(3, 2, HALF).transpose(1, 0, 2)
        blocks = jnp.broadcast_to(own[:, None], (2, 8, 3, HALF)).reshape(16, 3, HALF)
        got = exchange(blocks, "yl", "z").reshape(2, 24, HALF)
    with jax.named_scope("cotangent_x"):
        line = [got[0]] + [from_x(got[0], offset) for offset in (1, 2, 3)]
    with jax.named_scope("hidden_xy"):
        mine = exchange(jnp.broadcast_to(got[1], (16, 24, HALF)), "yl", "yh", "x").reshape(2, CORE_ROWS, HALF)
        line = jnp.concatenate(line, axis=0)
        head_mine, head_other, placed = small_call(
            onehots_kernel,
            "onehots",
            [((512, CORE_ROWS), jnp.bfloat16)] * 2 + [((2, 512, ROWS), jnp.bfloat16)],
            at,
            row_ids,
            head_orders,
            input_orders,
        )
        mine, line, table, at, head_mine, head_other, placed = lax.optimization_barrier(
            (mine, line, tied_table, at, head_mine, head_other, placed)
        )
        table = hold(table)
    with jax.named_scope("hidden_core"):
        other = other_core(mine)
    with jax.named_scope("cotangent_y"):
        own = [line] + [from_y(line, offset) for offset in (1, 2, 3)]
    with jax.named_scope("logits"):
        logits = [
            sum(
                lax.dot_general(
                    rows[i], half, (((1,), (1,)), ((), ())), preferred_element_type=jnp.float32
                )
                for i, half in enumerate((table[:, :HALF], table[:, HALF:]))
            )
            for rows in (mine, other)
        ]
    with jax.named_scope("stats"):
        (stats,) = small_call(stats_kernel, "stats", [((16, 4, CORE_ROWS), jnp.float32)], at, *logits)
        stats = exchange(stats, "z", "core")
        (stats,) = small_call(merge_kernel, "merge", [((16, 4, CORE_ROWS), jnp.float32)], stats)
        stats, own = lax.optimization_barrier((stats, own))
        far = [other_core(piece) for piece in own]
        stats = exchange(stats, "yl", "yh", "x")
    with jax.named_scope("coefficient"):
        *coefficient, turned_mine, turned_other = small_call(
            coefficient_kernel,
            "coefficient",
            [((CORE_ROWS, 512), jnp.bfloat16)] * 2,
            at,
            *logits,
            stats,
            head_mine,
            head_other,
            far_outs=[((512, CORE_ROWS), jnp.bfloat16)] * 2,
            scratch=[pltpu.VMEM((2, 512, CORE_ROWS), jnp.bfloat16), pltpu.SemaphoreType.DMA((2,))],
        )
        *coefficient, own, far = lax.optimization_barrier((*coefficient, own, far))
    with jax.named_scope("hidden_grad"):
        halves = (table[:, :HALF], table[:, HALF:])
        product = lambda rows, half: jnp.dot(rows, half, preferred_element_type=jnp.float32)
        theirs = [other_core(product(coefficient[1], half).astype(jnp.bfloat16)) for half in halves]
        ours = lax.optimization_barrier([product(coefficient[0], half) for half in halves])
        chip = jnp.stack([(a + b).astype(jnp.bfloat16) for a, b in zip(ours, theirs)])
    with jax.named_scope("hidden_grad"):
        plane = exchange(chip.reshape(16, 24, HALF), "yl", "yh", "x")
        plane, turned_mine, turned_other, own, far = lax.optimization_barrier(
            (plane, turned_mine, turned_other, own, far)
        )
        (plane,) = small_call(plane_kernel, "plane_sum", [((16, 3, HALF), jnp.bfloat16)], plane)
        last = exchange(plane, "yl", "z")
        table_grad = table_grad_call(at, turned_mine, turned_other, placed, mine, other, own, far)
        last, table_grad = lax.optimization_barrier((last, table_grad))
        last = jnp.sum(last.reshape(2, 8, 3, HALF).astype(jnp.float32), axis=1)
        hidden_grad = last.transpose(1, 0, 2).reshape(3, D).astype(jnp.bfloat16)
    return (table_grad, hidden_grad)


def solution(mesh):
    placed = (P("section", ("dp", "vocab"), None), P(("section", "dp", "vocab"), None), P())
    return jax.shard_map(
        shards,
        mesh=mesh,
        in_specs=placed,
        out_specs=(P(("section", "dp", "vocab"), None), P(("dp", "vocab"), None)),
        check_vma=False,
    )
```

```python
import math

import jax
import jax.numpy as jnp
from jax import lax
from jax.experimental import pallas as pl
from jax.experimental.pallas import tpu as pltpu
from jax.sharding import PartitionSpec as P

D = 4608
HALF = D // 2
ROWS = 384
CORE_ROWS = 192
CHUNK = 768
PER_HALF = HALF // CHUNK
AXES = ("section", "dp", "vocab")
SIZES = {"yl": 2, "yh": 2, "core": 2, "z": 8, "x": 4}
FACTOR = float(jnp.bfloat16(math.sqrt(D)))


def place(device):
    vocab, dp, section = device % 32, device // 32 % 4, device // 128
    return {"yl": section, "yh": dp // 2, "core": dp % 2, "z": vocab // 4, "x": vocab % 4}


def device_at(at):
    return (at["yl"] * 4 + at["yh"] * 2 + at["core"]) * 32 + at["z"] * 4 + at["x"]


def groups(*axes):
    found = {}
    for device in range(256):
        at = place(device)
        key = tuple(at[a] for a in SIZES if a not in axes)
        found.setdefault(key, []).append((tuple(at[a] for a in axes), device))
    return [[device for _, device in sorted(members)] for members in found.values()]


def exchange(blocks, *axes):
    return lax.all_to_all(blocks, AXES, 0, 0, axis_index_groups=groups(*axes), tiled=True)


def other_core(array):
    pairs = [pair for a, b in groups("core") for pair in ((a, b), (b, a))]
    return lax.ppermute(array, AXES, pairs)


def from_x(array, offset):
    pairs = []
    for device in range(256):
        at = place(device)
        pairs.append((device_at(dict(at, x=(at["x"] + offset) % 4)), device))
    return lax.ppermute(array, AXES, pairs)


def from_y(array, offset):
    pairs = []
    for device in range(256):
        at = place(device)
        y = (at["yh"] * 2 + at["yl"] + offset) % 4
        pairs.append((device_at(dict(at, yh=y // 2, yl=y % 2)), device))
    return lax.ppermute(array, AXES, pairs)


def natural_row(yh, core, z, x, j):
    return ((yh * 2 + core) * 32 + z * 4 + x) * 3 + j


def params(**more):
    return pltpu.CompilerParams(vmem_limit_bytes=14 * 2**20, **more)


def pick(condition, a, b):
    return jnp.where(condition, a, b)


def in_hbm(array):
    return pltpu.with_memory_space_constraint(array, pltpu.MemorySpace.HBM)


def hold_kernel(source, held, arrived):
    copy = pltpu.make_async_copy(source, held, arrived)
    copy.start()
    copy.wait()


def hold(array):
    return pl.pallas_call(
        hold_kernel,
        in_specs=[pl.BlockSpec(memory_space=pltpu.MemorySpace.HBM)],
        out_specs=pl.BlockSpec(memory_space=pltpu.VMEM),
        out_shape=pltpu.VMEM(array.shape, array.dtype),
        scratch_shapes=[pltpu.SemaphoreType.DMA],
        compiler_params=params(),
        name="hold",
    )(in_hbm(array))


def ids_onehot(ids, first, order, value):
    column = first + lax.broadcasted_iota(jnp.int32, (512, ROWS), 0)
    plain = jnp.where(column == ids, jnp.float32(value), jnp.float32(0)).astype(jnp.bfloat16)
    natural = lax.broadcasted_iota(jnp.int32, (ROWS, order.shape[1]), 0)
    move = jnp.where(natural == order, jnp.float32(1), jnp.float32(0)).astype(jnp.bfloat16)
    return jnp.dot(plain, move, preferred_element_type=jnp.float32)


HBM = pltpu.MemorySpace.HBM
SCALARS = pl.BlockSpec(memory_space=pltpu.SMEM)
BLOCK = pl.BlockSpec(memory_space=pltpu.VMEM)


def first_kernel(rows, out):
    for i in range(2):
        half = rows[0, :, i * HALF : (i + 1) * HALF]
        for k in range(8):
            out[8 * i + k] = half


def stats_kernel(at, mine, other, out):
    rows = []
    for logits in (mine, other):
        turned = logits[...].T
        high = jnp.max(turned, axis=0, keepdims=True)
        rows.append((high, jnp.sum(jnp.exp(turned - high), axis=0, keepdims=True)))
    first = at[0] == 0
    both = [pick(first, rows[i][k], rows[1 - i][k]) for k in range(2) for i in range(2)]
    out[...] = jnp.broadcast_to(jnp.concatenate(both, axis=0)[None], out.shape)


def merged(parts):
    high = jnp.max(parts[:, 0:2, :], axis=0)
    total = jnp.sum(parts[:, 2:4, :] * jnp.exp(parts[:, 0:2, :] - high), axis=0)
    return high, total


def merge_kernel(parts, out):
    out[...] = jnp.broadcast_to(jnp.concatenate(merged(parts[...]), axis=0)[None], out.shape)


def coefficient_kernel(at, mine, other, parts, head_mine, head_other, out_mine, out_other):
    high, total = merged(parts[...])
    scale = 1.0 / total
    first = at[0] == 0
    sides = ((mine, head_mine, out_mine), (other, head_other, out_other))
    for i, (logits, onehot, out) in enumerate(sides):
        top = pick(first, high[i : i + 1], high[1 - i : 2 - i])
        factor = pick(first, scale[i : i + 1], scale[1 - i : 2 - i])
        values = jnp.exp(logits[...].T - top) * factor - onehot[...].astype(jnp.float32)
        out[...] = values.T.astype(jnp.bfloat16)


def turn_kernel(mine, other, turned, kept, sent):
    kept[...] = jnp.concatenate([mine[...], other[...]], axis=0).T
    copy = pltpu.make_async_copy(kept, turned, sent)
    copy.start()
    copy.wait()


def onehots_kernel(at, ids, head_orders, input_orders, head_mine, head_other, placed):
    for i, out in enumerate((head_mine, head_other)):
        out[...] = ids_onehot(ids[1:2, :], at[2], head_orders[i : i + 1, :], 1.0).astype(jnp.bfloat16)
    for i in range(2):
        placed[i] = ids_onehot(ids[0:1, :], at[2], input_orders[i : i + 1, :], FACTOR).astype(jnp.bfloat16)


def plane_kernel(blocks, out):
    total = blocks[0].astype(jnp.float32)
    for i in range(1, blocks.shape[0]):
        total += blocks[i].astype(jnp.float32)
    for k in range(8):
        rows = total[3 * k : 3 * k + 3].astype(jnp.bfloat16)
        out[k] = rows
        out[8 + k] = rows


def small_call(kernel, name, outs, *args, far_outs=(), scratch=()):
    return pl.pallas_call(
        kernel,
        in_specs=[SCALARS if a.ndim == 1 else BLOCK for a in args],
        out_specs=[BLOCK] * len(outs) + [pl.BlockSpec(memory_space=HBM)] * len(far_outs),
        out_shape=[jax.ShapeDtypeStruct(*out) for out in outs] + [HBM(*out) for out in far_outs],
        scratch_shapes=scratch,
        compiler_params=params(),
        name=name,
    )(*args)


def table_grad_kernel(at, turned, placed, mine, other, *refs):
    own, far, (out, left, right, done, left_sem, right_sem, done_sem) = refs[:4], refs[4:8], refs[8:]
    lefts = []
    for part in range(2):
        for i, source in enumerate((turned, placed.at[part])):
            target = left.at[part, :, i * ROWS : (i + 1) * ROWS]
            lefts.append(pltpu.make_async_copy(source, target, left_sem.at[part, i]))

    def load(step):
        part, slot = step // PER_HALF, step % 2
        side = lax.bitwise_xor(at[1], part)
        columns = pl.ds(step % PER_HALF * CHUNK, CHUNK)
        sources = [mine.at[side, :, columns], other.at[side, :, columns]]
        sources += [rows[i].at[:, columns] for rows in (own, far) for i in (part, part + 2)]
        copies, begin = [], 0
        for i, source in enumerate(sources):
            rows = CORE_ROWS if i < 2 else 96
            copies.append(
                pltpu.make_async_copy(source, right.at[slot, begin : begin + rows, :], right_sem.at[slot, i])
            )
            begin += rows
        return copies

    def store(step):
        part, slot = step // PER_HALF, step % 2
        side = lax.bitwise_xor(at[1], part)
        begin = pl.multiple_of((side * PER_HALF + step % PER_HALF) * CHUNK, CHUNK)
        return pltpu.make_async_copy(done.at[slot], out.at[:, pl.ds(begin, CHUNK)], done_sem.at[slot])

    steps = 2 * PER_HALF
    loads, stores = [load(step) for step in range(steps)], [store(step) for step in range(steps)]
    for copy in lefts[:2] + loads[0] + lefts[2:]:
        copy.start()
    for step in range(steps):
        if step + 1 < steps:
            for copy in loads[step + 1]:
                copy.start()
        part, slot = step // PER_HALF, step % 2
        if step % PER_HALF == 0:
            for copy in lefts[2 * part : 2 * part + 2]:
                copy.wait()
        for copy in loads[step]:
            copy.wait()
        if step >= 2:
            stores[step - 2].wait()
        total = jnp.dot(left[part], right[slot], preferred_element_type=jnp.float32)
        done[slot] = total.astype(jnp.bfloat16)
        stores[step].start()
    for copy in stores[-2:]:
        copy.wait()


def table_grad_call(at, turned, placed, mine, other, own, far):
    arrays = [in_hbm(a) for a in (turned, placed, mine, other, *own, *far)]
    return pl.pallas_call(
        table_grad_kernel,
        in_specs=[SCALARS] + [pl.BlockSpec(memory_space=HBM)] * len(arrays),
        out_specs=pl.BlockSpec(memory_space=HBM),
        out_shape=jax.ShapeDtypeStruct((512, D), jnp.bfloat16),
        scratch_shapes=[
            pltpu.VMEM((2, 512, 2 * ROWS), jnp.bfloat16),
            pltpu.VMEM((2, 2 * ROWS, CHUNK), jnp.bfloat16),
            pltpu.VMEM((2, 512, CHUNK), jnp.bfloat16),
            pltpu.SemaphoreType.DMA((2, 2)),
            pltpu.SemaphoreType.DMA((2, 6)),
            pltpu.SemaphoreType.DMA((2,)),
        ],
        compiler_params=params(),
        cost_estimate=pl.CostEstimate(flops=4 * ROWS * 512 * D, bytes_accessed=13_000_000, transcendentals=0),
        name="table_grad",
    )(at, *arrays)


def shards(stacked_rows, tied_table, row_ids):
    section, dp, vocab = (lax.axis_index(a) for a in AXES)
    core, yh, x = dp % 2, dp // 2, vocab % 4
    first_column = ((section * 4 + dp) * 32 + vocab) * tied_table.shape[0]
    at = jnp.stack([core, section, first_column]).astype(jnp.int32)

    with jax.named_scope("orders"):
        i = lax.iota(jnp.int32, ROWS)
        c, yy, xx, z, j = i // 192, i // 96 % 2, i // 24 % 4, i // 3 % 8, i % 3
        moved_x = (x + xx) % 4
        y_of = lambda part: (yh * 2 + section + 2 * yy + part) % 4
        head_orders = natural_row(yy, lax.bitwise_xor(core, c), z, xx, j).reshape(2, CORE_ROWS)
        input_orders = jnp.stack(
            [natural_row(y_of(part) // 2, lax.bitwise_xor(core, c), z, moved_x, j) for part in range(2)]
        )

    with jax.named_scope("rows_lz"):
        (blocks,) = small_call(first_kernel, "first_blocks", [((16, 3, HALF), jnp.bfloat16)], stacked_rows)
        got = exchange(blocks, "yl", "z").reshape(2, 24, HALF)
    with jax.named_scope("cotangent_x"):
        line = [got[0]] + [from_x(got[0], offset) for offset in (1, 2, 3)]
    with jax.named_scope("hidden_xy"):
        mine = exchange(jnp.broadcast_to(got[1], (16, 24, HALF)), "yl", "yh", "x").reshape(2, CORE_ROWS, HALF)
        line = jnp.concatenate(line, axis=0)
        head_mine, head_other, placed = small_call(
            onehots_kernel,
            "onehots",
            [((512, CORE_ROWS), jnp.bfloat16)] * 2 + [((2, 512, ROWS), jnp.bfloat16)],
            at,
            row_ids,
            head_orders,
            input_orders,
        )
        mine, line, table, at, head_mine, head_other, placed = lax.optimization_barrier(
            (mine, line, tied_table, at, head_mine, head_other, placed)
        )
        table = hold(table)
    with jax.named_scope("hidden_core"):
        other = other_core(mine)
    with jax.named_scope("cotangent_y"):
        own = [line] + [from_y(line, offset) for offset in (1, 2, 3)]
    with jax.named_scope("logits"):
        logits = [
            sum(
                lax.dot_general(
                    rows[i], half, (((1,), (1,)), ((), ())), preferred_element_type=jnp.float32
                )
                for i, half in enumerate((table[:, :HALF], table[:, HALF:]))
            )
            for rows in (mine, other)
        ]
    with jax.named_scope("stats"):
        (stats,) = small_call(stats_kernel, "stats", [((16, 4, CORE_ROWS), jnp.float32)], at, *logits)
        stats = exchange(stats, "z", "core")
        (stats,) = small_call(merge_kernel, "merge", [((16, 4, CORE_ROWS), jnp.float32)], stats)
        stats, own = lax.optimization_barrier((stats, own))
        far = [other_core(piece) for piece in own]
        stats = exchange(stats, "yl", "yh", "x")
    with jax.named_scope("coefficient"):
        coefficient = small_call(
            coefficient_kernel,
            "coefficient",
            [((CORE_ROWS, 512), jnp.bfloat16)] * 2,
            at,
            *logits,
            stats,
            head_mine,
            head_other,
        )
        *coefficient, own, far = lax.optimization_barrier((*coefficient, own, far))
    with jax.named_scope("hidden_grad"):
        halves = (table[:, :HALF], table[:, HALF:])
        product = lambda rows, half: jnp.dot(rows, half, preferred_element_type=jnp.float32)
        theirs = [other_core(product(coefficient[1], half).astype(jnp.bfloat16)) for half in halves]
        ours = lax.optimization_barrier([product(coefficient[0], half) for half in halves])
        chip = jnp.stack([(a + b).astype(jnp.bfloat16) for a, b in zip(ours, theirs)])
    with jax.named_scope("hidden_grad"):
        (turned,) = small_call(
            turn_kernel,
            "turn",
            [],
            *coefficient,
            far_outs=[((512, ROWS), jnp.bfloat16)],
            scratch=[pltpu.VMEM((512, ROWS), jnp.bfloat16), pltpu.SemaphoreType.DMA],
        )
        chip, turned = lax.optimization_barrier((chip, turned))
        plane = exchange(chip.reshape(16, 24, HALF), "yl", "yh", "x")
        plane, turned, own, far = lax.optimization_barrier((plane, turned, own, far))
        (plane,) = small_call(plane_kernel, "plane_sum", [((16, 3, HALF), jnp.bfloat16)], plane)
        last = exchange(plane, "yl", "z")
        table_grad = table_grad_call(at, turned, placed, mine, other, own, far)
        last, table_grad = lax.optimization_barrier((last, table_grad))
        last = jnp.sum(last.reshape(2, 8, 3, HALF).astype(jnp.float32), axis=1)
        hidden_grad = last.transpose(1, 0, 2).reshape(3, D).astype(jnp.bfloat16)
    return (table_grad, hidden_grad)


def solution(mesh):
    placed = (P("section", ("dp", "vocab"), None), P(("section", "dp", "vocab"), None), P())
    return jax.shard_map(
        shards,
        mesh=mesh,
        in_specs=placed,
        out_specs=(P(("section", "dp", "vocab"), None), P(("dp", "vocab"), None)),
        check_vma=False,
    )
```

```python
import math

import jax
import jax.numpy as jnp
from jax import lax
from jax.experimental import pallas as pl
from jax.experimental.pallas import tpu as pltpu
from jax.sharding import PartitionSpec as P

D = 4608
HALF = D // 2
ROWS = 384
CORE_ROWS = 192
CHUNK = 768
PER_HALF = HALF // CHUNK
AXES = ("section", "dp", "vocab")
SIZES = {"yl": 2, "yh": 2, "core": 2, "z": 8, "x": 4}
FACTOR = float(jnp.bfloat16(math.sqrt(D)))


def place(device):
    vocab, dp, section = device % 32, device // 32 % 4, device // 128
    return {"yl": section, "yh": dp // 2, "core": dp % 2, "z": vocab // 4, "x": vocab % 4}


def device_at(at):
    return (at["yl"] * 4 + at["yh"] * 2 + at["core"]) * 32 + at["z"] * 4 + at["x"]


def groups(*axes):
    found = {}
    for device in range(256):
        at = place(device)
        key = tuple(at[a] for a in SIZES if a not in axes)
        found.setdefault(key, []).append((tuple(at[a] for a in axes), device))
    return [[device for _, device in sorted(members)] for members in found.values()]


def exchange(blocks, *axes):
    return lax.all_to_all(blocks, AXES, 0, 0, axis_index_groups=groups(*axes), tiled=True)


def other_core(array):
    pairs = [pair for a, b in groups("core") for pair in ((a, b), (b, a))]
    return lax.ppermute(array, AXES, pairs)


def from_x(array, offset):
    pairs = []
    for device in range(256):
        at = place(device)
        pairs.append((device_at(dict(at, x=(at["x"] + offset) % 4)), device))
    return lax.ppermute(array, AXES, pairs)


def from_y(array, offset):
    pairs = []
    for device in range(256):
        at = place(device)
        y = (at["yh"] * 2 + at["yl"] + offset) % 4
        pairs.append((device_at(dict(at, yh=y // 2, yl=y % 2)), device))
    return lax.ppermute(array, AXES, pairs)


def natural_row(yh, core, z, x, j):
    return ((yh * 2 + core) * 32 + z * 4 + x) * 3 + j


def params(**more):
    return pltpu.CompilerParams(vmem_limit_bytes=14 * 2**20, **more)


def pick(condition, a, b):
    return jnp.where(condition, a, b)


def in_hbm(array):
    return pltpu.with_memory_space_constraint(array, pltpu.MemorySpace.HBM)


def hold_kernel(source, held, arrived):
    copies = []
    for i in range(8):
        rows = slice(64 * i, 64 * i + 64)
        copies.append(pltpu.make_async_copy(source.at[rows, :], held.at[rows, :], arrived.at[i]))
        copies[-1].start()
    for copy in copies:
        copy.wait()


def hold(array):
    return pl.pallas_call(
        hold_kernel,
        in_specs=[pl.BlockSpec(memory_space=pltpu.MemorySpace.HBM)],
        out_specs=pl.BlockSpec(memory_space=pltpu.VMEM),
        out_shape=pltpu.VMEM(array.shape, array.dtype),
        scratch_shapes=[pltpu.SemaphoreType.DMA((8,))],
        compiler_params=params(),
        name="hold",
    )(in_hbm(array))


def ids_onehot(ids, first, order, value):
    column = first + lax.broadcasted_iota(jnp.int32, (512, ROWS), 0)
    plain = jnp.where(column == ids, jnp.float32(value), jnp.float32(0)).astype(jnp.bfloat16)
    natural = lax.broadcasted_iota(jnp.int32, (ROWS, order.shape[1]), 0)
    move = jnp.where(natural == order, jnp.float32(1), jnp.float32(0)).astype(jnp.bfloat16)
    return jnp.dot(plain, move, preferred_element_type=jnp.float32)


HBM = pltpu.MemorySpace.HBM
SCALARS = pl.BlockSpec(memory_space=pltpu.SMEM)
BLOCK = pl.BlockSpec(memory_space=pltpu.VMEM)


def fold(rows):
    top = jnp.concatenate([rows[0:1], rows[1:2, : HALF // 2]], axis=1)
    return jnp.concatenate([top, jnp.concatenate([rows[1:2, HALF // 2 :], rows[2:3]], axis=1)], axis=0)


def unfold(pair):
    middle = jnp.concatenate([pair[0:1, HALF:], pair[1:2, : HALF // 2]], axis=1)
    return jnp.concatenate([pair[0:1, :HALF], middle, pair[1:2, HALF // 2 :]], axis=0)


def first_kernel(rows, out):
    for i in range(2):
        half = fold(rows[0, :, i * HALF : (i + 1) * HALF].astype(jnp.float32)).astype(jnp.bfloat16)
        for k in range(8):
            out[8 * i + k] = half


def last_kernel(blocks, out):
    for i in range(2):
        total = blocks[8 * i].astype(jnp.float32)
        for k in range(1, 8):
            total += blocks[8 * i + k].astype(jnp.float32)
        out[:, i * HALF : (i + 1) * HALF] = unfold(total).astype(jnp.bfloat16)


def rows_kernel(got, cotangent, blocks, hidden, sent):
    merge = lambda begin: jnp.concatenate([unfold(got[begin + k].astype(jnp.float32)) for k in range(8)], axis=0)
    hidden[...] = merge(8).astype(jnp.bfloat16)
    copies = []
    for i in range(16):
        copies.append(pltpu.make_async_copy(hidden, blocks.at[i], sent.at[i]))
        copies[-1].start()
    cotangent[...] = merge(0).astype(jnp.bfloat16)
    for copy in copies:
        copy.wait()


def stats_kernel(at, mine, other, out):
    rows = []
    for logits in (mine, other):
        turned = logits[...].T
        high = jnp.max(turned, axis=0, keepdims=True)
        rows.append((high, jnp.sum(jnp.exp(turned - high), axis=0, keepdims=True)))
    first = at[0] == 0
    both = [pick(first, rows[i][k], rows[1 - i][k]) for k in range(2) for i in range(2)]
    out[...] = jnp.broadcast_to(jnp.concatenate(both, axis=0)[None], out.shape)


def merged(parts):
    high = jnp.max(parts[:, 0:2, :], axis=0)
    total = jnp.sum(parts[:, 2:4, :] * jnp.exp(parts[:, 0:2, :] - high), axis=0)
    return high, total


def merge_kernel(parts, out):
    out[...] = jnp.broadcast_to(jnp.concatenate(merged(parts[...]), axis=0)[None], out.shape)


def coefficient_kernel(at, mine, other, parts, head_mine, head_other, out_mine, out_other):
    high, total = merged(parts[...])
    scale = 1.0 / total
    first = at[0] == 0
    sides = ((mine, head_mine, out_mine), (other, head_other, out_other))
    for i, (logits, onehot, out) in enumerate(sides):
        top = pick(first, high[i : i + 1], high[1 - i : 2 - i])
        factor = pick(first, scale[i : i + 1], scale[1 - i : 2 - i])
        values = jnp.exp(logits[...].T - top) * factor - onehot[...].astype(jnp.float32)
        out[...] = values.T.astype(jnp.bfloat16)


def turn_kernel(mine, other, turned, kept, sent):
    kept[...] = jnp.concatenate([mine[...], other[...]], axis=0).T
    copy = pltpu.make_async_copy(kept, turned, sent)
    copy.start()
    copy.wait()


def onehots_kernel(at, ids, head_orders, input_orders, head_mine, head_other, placed):
    for i, out in enumerate((head_mine, head_other)):
        out[...] = ids_onehot(ids[1:2, :], at[2], head_orders[i : i + 1, :], 1.0).astype(jnp.bfloat16)
    for i in range(2):
        placed[i] = ids_onehot(ids[0:1, :], at[2], input_orders[i : i + 1, :], FACTOR).astype(jnp.bfloat16)


def plane_kernel(blocks, out):
    total = blocks[0].astype(jnp.float32)
    for i in range(1, blocks.shape[0]):
        total += blocks[i].astype(jnp.float32)
    for k in range(8):
        rows = fold(total[3 * k : 3 * k + 3]).astype(jnp.bfloat16)
        out[k] = rows
        out[8 + k] = rows


def small_call(kernel, name, outs, *args, far_outs=(), scratch=()):
    return pl.pallas_call(
        kernel,
        in_specs=[SCALARS if a.ndim == 1 else BLOCK for a in args],
        out_specs=[BLOCK] * len(outs) + [pl.BlockSpec(memory_space=HBM)] * len(far_outs),
        out_shape=[jax.ShapeDtypeStruct(*out) for out in outs] + [HBM(*out) for out in far_outs],
        scratch_shapes=scratch,
        compiler_params=params(),
        name=name,
    )(*args)


def table_grad_kernel(at, turned, placed, mine, other, *refs):
    own, far, (out, left, right, done, left_sem, right_sem, done_sem) = refs[:4], refs[4:8], refs[8:]
    lefts = []
    for part in range(2):
        for i, source in enumerate((turned, placed.at[part])):
            target = left.at[part, :, i * ROWS : (i + 1) * ROWS]
            lefts.append(pltpu.make_async_copy(source, target, left_sem.at[part, i]))

    def load(step):
        part, slot = step // PER_HALF, step % 2
        side = lax.bitwise_xor(at[1], part)
        columns = pl.ds(step % PER_HALF * CHUNK, CHUNK)
        sources = [mine.at[side, :, columns], other.at[side, :, columns]]
        sources += [rows[i].at[:, columns] for rows in (own, far) for i in (part, part + 2)]
        copies, begin = [], 0
        for i, source in enumerate(sources):
            rows = CORE_ROWS if i < 2 else 96
            copies.append(
                pltpu.make_async_copy(source, right.at[slot, begin : begin + rows, :], right_sem.at[slot, i])
            )
            begin += rows
        return copies

    def store(step):
        part, slot = step // PER_HALF, step % 2
        side = lax.bitwise_xor(at[1], part)
        begin = pl.multiple_of((side * PER_HALF + step % PER_HALF) * CHUNK, CHUNK)
        return pltpu.make_async_copy(done.at[slot], out.at[:, pl.ds(begin, CHUNK)], done_sem.at[slot])

    steps = 2 * PER_HALF
    loads, stores = [load(step) for step in range(steps)], [store(step) for step in range(steps)]
    for copy in lefts[:2] + loads[0] + lefts[2:]:
        copy.start()
    for step in range(steps):
        if step + 1 < steps:
            for copy in loads[step + 1]:
                copy.start()
        part, slot = step // PER_HALF, step % 2
        if step % PER_HALF == 0:
            for copy in lefts[2 * part : 2 * part + 2]:
                copy.wait()
        for copy in loads[step]:
            copy.wait()
        if step >= 2:
            stores[step - 2].wait()
        total = jnp.dot(left[part], right[slot], preferred_element_type=jnp.float32)
        done[slot] = total.astype(jnp.bfloat16)
        stores[step].start()
    for copy in stores[-2:]:
        copy.wait()


def table_grad_call(at, turned, placed, mine, other, own, far):
    arrays = [in_hbm(a) for a in (turned, placed, mine, other, *own, *far)]
    return pl.pallas_call(
        table_grad_kernel,
        in_specs=[SCALARS] + [pl.BlockSpec(memory_space=HBM)] * len(arrays),
        out_specs=pl.BlockSpec(memory_space=HBM),
        out_shape=jax.ShapeDtypeStruct((512, D), jnp.bfloat16),
        scratch_shapes=[
            pltpu.VMEM((2, 512, 2 * ROWS), jnp.bfloat16),
            pltpu.VMEM((2, 2 * ROWS, CHUNK), jnp.bfloat16),
            pltpu.VMEM((2, 512, CHUNK), jnp.bfloat16),
            pltpu.SemaphoreType.DMA((2, 2)),
            pltpu.SemaphoreType.DMA((2, 6)),
            pltpu.SemaphoreType.DMA((2,)),
        ],
        compiler_params=params(),
        cost_estimate=pl.CostEstimate(flops=4 * ROWS * 512 * D, bytes_accessed=13_000_000, transcendentals=0),
        name="table_grad",
    )(at, *arrays)


def shards(stacked_rows, tied_table, row_ids):
    section, dp, vocab = (lax.axis_index(a) for a in AXES)
    core, yh, x = dp % 2, dp // 2, vocab % 4
    first_column = ((section * 4 + dp) * 32 + vocab) * tied_table.shape[0]
    at = jnp.stack([core, section, first_column]).astype(jnp.int32)

    with jax.named_scope("orders"):
        i = lax.iota(jnp.int32, ROWS)
        c, yy, xx, z, j = i // 192, i // 96 % 2, i // 24 % 4, i // 3 % 8, i % 3
        moved_x = (x + xx) % 4
        y_of = lambda part: (yh * 2 + section + 2 * yy + part) % 4
        head_orders = natural_row(yy, lax.bitwise_xor(core, c), z, xx, j).reshape(2, CORE_ROWS)
        input_orders = jnp.stack(
            [natural_row(y_of(part) // 2, lax.bitwise_xor(core, c), z, moved_x, j) for part in range(2)]
        )

    with jax.named_scope("rows_lz"):
        (blocks,) = small_call(first_kernel, "first_blocks", [((16, 2, 3 * HALF // 2), jnp.bfloat16)], stacked_rows)
        cotangent, blocks = small_call(
            rows_kernel,
            "rows",
            [((24, HALF), jnp.bfloat16)],
            exchange(blocks, "yl", "z"),
            far_outs=[((16, 24, HALF), jnp.bfloat16)],
            scratch=[pltpu.VMEM((24, HALF), jnp.bfloat16), pltpu.SemaphoreType.DMA((16,))],
        )
    with jax.named_scope("cotangent_x"):
        line = [cotangent] + [from_x(cotangent, offset) for offset in (1, 2, 3)]
    with jax.named_scope("hidden_xy"):
        mine = exchange(blocks, "yl", "yh", "x").reshape(2, CORE_ROWS, HALF)
        line = jnp.concatenate(line, axis=0)
        head_mine, head_other, placed = small_call(
            onehots_kernel,
            "onehots",
            [((512, CORE_ROWS), jnp.bfloat16)] * 2 + [((2, 512, ROWS), jnp.bfloat16)],
            at,
            row_ids,
            head_orders,
            input_orders,
        )
        mine, line, table, at, head_mine, head_other, placed = lax.optimization_barrier(
            (mine, line, tied_table, at, head_mine, head_other, placed)
        )
        table = hold(table)
    with jax.named_scope("hidden_core"):
        other = other_core(mine)
    with jax.named_scope("cotangent_y"):
        own = [line] + [from_y(line, offset) for offset in (1, 2, 3)]
    with jax.named_scope("logits"):
        logits = [
            sum(
                lax.dot_general(
                    rows[i], half, (((1,), (1,)), ((), ())), preferred_element_type=jnp.float32
                )
                for i, half in enumerate((table[:, :HALF], table[:, HALF:]))
            )
            for rows in (mine, other)
        ]
    with jax.named_scope("stats"):
        (stats,) = small_call(stats_kernel, "stats", [((16, 4, CORE_ROWS), jnp.float32)], at, *logits)
        stats = exchange(stats, "z", "core")
        (stats,) = small_call(merge_kernel, "merge", [((16, 4, CORE_ROWS), jnp.float32)], stats)
        stats, own = lax.optimization_barrier((stats, own))
        far = [other_core(piece) for piece in own]
        stats = exchange(stats, "yl", "yh", "x")
    with jax.named_scope("coefficient"):
        coefficient = small_call(
            coefficient_kernel,
            "coefficient",
            [((CORE_ROWS, 512), jnp.bfloat16)] * 2,
            at,
            *logits,
            stats,
            head_mine,
            head_other,
        )
        *coefficient, own, far = lax.optimization_barrier((*coefficient, own, far))
    with jax.named_scope("hidden_grad"):
        halves = (table[:, :HALF], table[:, HALF:])
        product = lambda rows, half: jnp.dot(rows, half, preferred_element_type=jnp.float32)
        theirs = [other_core(product(coefficient[1], half).astype(jnp.bfloat16)) for half in halves]
        ours = lax.optimization_barrier([product(coefficient[0], half) for half in halves])
        chip = jnp.stack([(a + b).astype(jnp.bfloat16) for a, b in zip(ours, theirs)])
    with jax.named_scope("hidden_grad"):
        (turned,) = small_call(
            turn_kernel,
            "turn",
            [],
            *coefficient,
            far_outs=[((512, ROWS), jnp.bfloat16)],
            scratch=[pltpu.VMEM((512, ROWS), jnp.bfloat16), pltpu.SemaphoreType.DMA],
        )
        chip, turned = lax.optimization_barrier((chip, turned))
        plane = exchange(chip.reshape(16, 24, HALF), "yl", "yh", "x")
        plane, turned, own, far = lax.optimization_barrier((plane, turned, own, far))
        (plane,) = small_call(plane_kernel, "plane_sum", [((16, 2, 3 * HALF // 2), jnp.bfloat16)], plane)
        last = exchange(plane, "yl", "z")
        table_grad = table_grad_call(at, turned, placed, mine, other, own, far)
        last, table_grad = lax.optimization_barrier((last, table_grad))
        (hidden_grad,) = small_call(last_kernel, "last_sum", [((3, D), jnp.bfloat16)], last)
    return (table_grad, hidden_grad)


def solution(mesh):
    placed = (P("section", ("dp", "vocab"), None), P(("section", "dp", "vocab"), None), P())
    return jax.shard_map(
        shards,
        mesh=mesh,
        in_specs=placed,
        out_specs=(P(("section", "dp", "vocab"), None), P(("dp", "vocab"), None)),
        check_vma=False,
    )
```

```python
import math

import jax
import jax.numpy as jnp
from jax import lax
from jax.experimental import pallas as pl
from jax.experimental.pallas import tpu as pltpu
from jax.sharding import PartitionSpec as P

D = 4608
HALF = D // 2
ROWS = 384
CORE_ROWS = 192
CHUNK = 768
PER_HALF = HALF // CHUNK
AXES = ("section", "dp", "vocab")
SIZES = {"yl": 2, "yh": 2, "core": 2, "z": 8, "x": 4}
FACTOR = float(jnp.bfloat16(math.sqrt(D)))


def place(device):
    vocab, dp, section = device % 32, device // 32 % 4, device // 128
    return {"yl": section, "yh": dp // 2, "core": dp % 2, "z": vocab // 4, "x": vocab % 4}


def device_at(at):
    return (at["yl"] * 4 + at["yh"] * 2 + at["core"]) * 32 + at["z"] * 4 + at["x"]


def groups(*axes):
    found = {}
    for device in range(256):
        at = place(device)
        key = tuple(at[a] for a in SIZES if a not in axes)
        found.setdefault(key, []).append((tuple(at[a] for a in axes), device))
    return [[device for _, device in sorted(members)] for members in found.values()]


def exchange(blocks, *axes):
    return lax.all_to_all(blocks, AXES, 0, 0, axis_index_groups=groups(*axes), tiled=True)


def other_core(array):
    pairs = [pair for a, b in groups("core") for pair in ((a, b), (b, a))]
    return lax.ppermute(array, AXES, pairs)


def from_x(array, offset):
    pairs = []
    for device in range(256):
        at = place(device)
        pairs.append((device_at(dict(at, x=(at["x"] + offset) % 4)), device))
    return lax.ppermute(array, AXES, pairs)


def from_y(array, offset):
    pairs = []
    for device in range(256):
        at = place(device)
        y = (at["yh"] * 2 + at["yl"] + offset) % 4
        pairs.append((device_at(dict(at, yh=y // 2, yl=y % 2)), device))
    return lax.ppermute(array, AXES, pairs)


def natural_row(yh, core, z, x, j):
    return ((yh * 2 + core) * 32 + z * 4 + x) * 3 + j


def params(**more):
    return pltpu.CompilerParams(vmem_limit_bytes=14 * 2**20, **more)


def pick(condition, a, b):
    return jnp.where(condition, a, b)


def in_hbm(array):
    return pltpu.with_memory_space_constraint(array, pltpu.MemorySpace.HBM)


def hold_kernel(source, held, arrived):
    copies = []
    for i in range(8):
        rows = slice(64 * i, 64 * i + 64)
        copies.append(pltpu.make_async_copy(source.at[rows, :], held.at[rows, :], arrived.at[i]))
        copies[-1].start()
    for copy in copies:
        copy.wait()


def hold(array):
    return pl.pallas_call(
        hold_kernel,
        in_specs=[pl.BlockSpec(memory_space=pltpu.MemorySpace.HBM)],
        out_specs=pl.BlockSpec(memory_space=pltpu.VMEM),
        out_shape=pltpu.VMEM(array.shape, array.dtype),
        scratch_shapes=[pltpu.SemaphoreType.DMA((8,))],
        compiler_params=params(),
        name="hold",
    )(in_hbm(array))


def ids_onehot(ids, first, order, value):
    column = first + lax.broadcasted_iota(jnp.int32, (512, ROWS), 0)
    plain = jnp.where(column == ids, jnp.float32(value), jnp.float32(0)).astype(jnp.bfloat16)
    natural = lax.broadcasted_iota(jnp.int32, (ROWS, order.shape[1]), 0)
    move = jnp.where(natural == order, jnp.float32(1), jnp.float32(0)).astype(jnp.bfloat16)
    return jnp.dot(plain, move, preferred_element_type=jnp.float32)


HBM = pltpu.MemorySpace.HBM
SCALARS = pl.BlockSpec(memory_space=pltpu.SMEM)
BLOCK = pl.BlockSpec(memory_space=pltpu.VMEM)


def fold(rows):
    top = jnp.concatenate([rows[0:1], rows[1:2, : HALF // 2]], axis=1)
    return jnp.concatenate([top, jnp.concatenate([rows[1:2, HALF // 2 :], rows[2:3]], axis=1)], axis=0)


def unfold(pair):
    middle = jnp.concatenate([pair[0:1, HALF:], pair[1:2, : HALF // 2]], axis=1)
    return jnp.concatenate([pair[0:1, :HALF], middle, pair[1:2, HALF // 2 :]], axis=0)


def first_kernel(rows, out):
    for i in range(2):
        half = fold(rows[0, :, i * HALF : (i + 1) * HALF].astype(jnp.float32)).astype(jnp.bfloat16)
        for k in range(8):
            out[8 * i + k] = half


def last_kernel(blocks, out):
    for i in range(2):
        total = blocks[8 * i].astype(jnp.float32)
        for k in range(1, 8):
            total += blocks[8 * i + k].astype(jnp.float32)
        out[:, i * HALF : (i + 1) * HALF] = unfold(total).astype(jnp.bfloat16)


def rows_kernel(got, cotangent, blocks, hidden, sent):
    merge = lambda begin: jnp.concatenate([unfold(got[begin + k].astype(jnp.float32)) for k in range(8)], axis=0)
    hidden[...] = merge(8).astype(jnp.bfloat16)
    copies = []
    for i in range(16):
        copies.append(pltpu.make_async_copy(hidden, blocks.at[i], sent.at[i]))
        copies[-1].start()
    cotangent[...] = merge(0).astype(jnp.bfloat16)
    for copy in copies:
        copy.wait()


def stats_kernel(at, mine, other, out):
    rows = []
    for logits in (mine, other):
        turned = logits[...].T
        high = jnp.max(turned, axis=0, keepdims=True)
        rows.append((high, jnp.sum(jnp.exp(turned - high), axis=0, keepdims=True)))
    first = at[0] == 0
    both = [pick(first, rows[i][k], rows[1 - i][k]) for k in range(2) for i in range(2)]
    out[...] = jnp.broadcast_to(jnp.concatenate(both, axis=0)[None], out.shape)


def merged(parts):
    high = jnp.max(parts[:, 0:2, :], axis=0)
    total = jnp.sum(parts[:, 2:4, :] * jnp.exp(parts[:, 0:2, :] - high), axis=0)
    return high, total


def merge_kernel(parts, out):
    out[...] = jnp.broadcast_to(jnp.concatenate(merged(parts[...]), axis=0)[None], out.shape)


def coefficient_kernel(at, mine, other, parts, head_mine, head_other, out_mine, out_other):
    high, total = merged(parts[...])
    scale = 1.0 / total
    first = at[0] == 0
    sides = ((mine, head_mine, out_mine), (other, head_other, out_other))
    for i, (logits, onehot, out) in enumerate(sides):
        top = pick(first, high[i : i + 1], high[1 - i : 2 - i])
        factor = pick(first, scale[i : i + 1], scale[1 - i : 2 - i])
        values = jnp.exp(logits[...].T - top) * factor - onehot[...].astype(jnp.float32)
        out[...] = values.T.astype(jnp.bfloat16)


def turn_kernel(mine, other, turned, kept, sent):
    kept[...] = jnp.concatenate([mine[...], other[...]], axis=0).T
    copy = pltpu.make_async_copy(kept, turned, sent)
    copy.start()
    copy.wait()


def onehots_kernel(at, ids, head_orders, input_orders, head_mine, head_other, placed):
    for i, out in enumerate((head_mine, head_other)):
        out[...] = ids_onehot(ids[1:2, :], at[2], head_orders[i : i + 1, :], 1.0).astype(jnp.bfloat16)
    for i in range(2):
        placed[i] = ids_onehot(ids[0:1, :], at[2], input_orders[i : i + 1, :], FACTOR).astype(jnp.bfloat16)


def plane_kernel(blocks, out):
    total = blocks[0].astype(jnp.float32)
    for i in range(1, blocks.shape[0]):
        total += blocks[i].astype(jnp.float32)
    for k in range(8):
        rows = fold(total[3 * k : 3 * k + 3]).astype(jnp.bfloat16)
        out[k] = rows
        out[8 + k] = rows


def small_call(kernel, name, outs, *args, far_outs=(), scratch=()):
    return pl.pallas_call(
        kernel,
        in_specs=[SCALARS if a.ndim == 1 else BLOCK for a in args],
        out_specs=[BLOCK] * len(outs) + [pl.BlockSpec(memory_space=HBM)] * len(far_outs),
        out_shape=[jax.ShapeDtypeStruct(*out) for out in outs] + [HBM(*out) for out in far_outs],
        scratch_shapes=scratch,
        compiler_params=params(),
        name=name,
    )(*args)


def table_grad_kernel(at, turned, placed, mine, other, *refs):
    own, far, (out, left, right, done, left_sem, right_sem, done_sem) = refs[:4], refs[4:8], refs[8:]
    lefts = []
    for part in range(2):
        for i, source in enumerate((turned, placed.at[part])):
            target = left.at[part, :, i * ROWS : (i + 1) * ROWS]
            lefts.append(pltpu.make_async_copy(source, target, left_sem.at[part, i]))

    def load(step):
        part, slot = step // PER_HALF, step % 2
        side = lax.bitwise_xor(at[1], part)
        columns = pl.ds(step % PER_HALF * CHUNK, CHUNK)
        sources = [mine.at[side, :, columns], other.at[side, :, columns]]
        sources += [rows[i].at[:, columns] for rows in (own, far) for i in (part, part + 2)]
        copies, begin = [], 0
        for i, source in enumerate(sources):
            rows = CORE_ROWS if i < 2 else 96
            copies.append(
                pltpu.make_async_copy(source, right.at[slot, begin : begin + rows, :], right_sem.at[slot, i])
            )
            begin += rows
        return copies

    def store(step):
        part, slot = step // PER_HALF, step % 2
        side = lax.bitwise_xor(at[1], part)
        begin = pl.multiple_of((side * PER_HALF + step % PER_HALF) * CHUNK, CHUNK)
        return pltpu.make_async_copy(done.at[slot], out.at[:, pl.ds(begin, CHUNK)], done_sem.at[slot])

    steps = 2 * PER_HALF
    loads, stores = [load(step) for step in range(steps)], [store(step) for step in range(steps)]
    for copy in lefts[:2] + loads[0]:
        copy.start()
    for step in range(steps):
        if step + 1 < steps:
            for copy in loads[step + 1] + (lefts[2:] if step == 1 else []):
                copy.start()
        part, slot = step // PER_HALF, step % 2
        if step % PER_HALF == 0:
            for copy in lefts[2 * part : 2 * part + 2]:
                copy.wait()
        for copy in loads[step]:
            copy.wait()
        if step >= 2:
            stores[step - 2].wait()
        total = jnp.dot(left[part], right[slot], preferred_element_type=jnp.float32)
        done[slot] = total.astype(jnp.bfloat16)
        stores[step].start()
    for copy in stores[-2:]:
        copy.wait()


def table_grad_call(at, turned, placed, mine, other, own, far):
    arrays = [in_hbm(a) for a in (turned, placed, mine, other, *own, *far)]
    return pl.pallas_call(
        table_grad_kernel,
        in_specs=[SCALARS] + [pl.BlockSpec(memory_space=HBM)] * len(arrays),
        out_specs=pl.BlockSpec(memory_space=HBM),
        out_shape=jax.ShapeDtypeStruct((512, D), jnp.bfloat16),
        scratch_shapes=[
            pltpu.VMEM((2, 512, 2 * ROWS), jnp.bfloat16),
            pltpu.VMEM((2, 2 * ROWS, CHUNK), jnp.bfloat16),
            pltpu.VMEM((2, 512, CHUNK), jnp.bfloat16),
            pltpu.SemaphoreType.DMA((2, 2)),
            pltpu.SemaphoreType.DMA((2, 6)),
            pltpu.SemaphoreType.DMA((2,)),
        ],
        compiler_params=params(),
        cost_estimate=pl.CostEstimate(flops=4 * ROWS * 512 * D, bytes_accessed=13_000_000, transcendentals=0),
        name="table_grad",
    )(at, *arrays)


def shards(stacked_rows, tied_table, row_ids):
    section, dp, vocab = (lax.axis_index(a) for a in AXES)
    core, yh, x = dp % 2, dp // 2, vocab % 4
    first_column = ((section * 4 + dp) * 32 + vocab) * tied_table.shape[0]
    at = jnp.stack([core, section, first_column]).astype(jnp.int32)

    with jax.named_scope("orders"):
        i = lax.iota(jnp.int32, ROWS)
        c, yy, xx, z, j = i // 192, i // 96 % 2, i // 24 % 4, i // 3 % 8, i % 3
        moved_x = (x + xx) % 4
        y_of = lambda part: (yh * 2 + section + 2 * yy + part) % 4
        head_orders = natural_row(yy, lax.bitwise_xor(core, c), z, xx, j).reshape(2, CORE_ROWS)
        input_orders = jnp.stack(
            [natural_row(y_of(part) // 2, lax.bitwise_xor(core, c), z, moved_x, j) for part in range(2)]
        )

    with jax.named_scope("rows_lz"):
        (blocks,) = small_call(first_kernel, "first_blocks", [((16, 2, 3 * HALF // 2), jnp.bfloat16)], stacked_rows)
        cotangent, blocks = small_call(
            rows_kernel,
            "rows",
            [((24, HALF), jnp.bfloat16)],
            exchange(blocks, "yl", "z"),
            far_outs=[((16, 24, HALF), jnp.bfloat16)],
            scratch=[pltpu.VMEM((24, HALF), jnp.bfloat16), pltpu.SemaphoreType.DMA((16,))],
        )
    with jax.named_scope("cotangent_x"):
        line = [cotangent] + [from_x(cotangent, offset) for offset in (1, 2, 3)]
    with jax.named_scope("hidden_xy"):
        mine = exchange(blocks, "yl", "yh", "x").reshape(2, CORE_ROWS, HALF)
        line = jnp.concatenate(line, axis=0)
        head_mine, head_other, placed = small_call(
            onehots_kernel,
            "onehots",
            [((512, CORE_ROWS), jnp.bfloat16)] * 2 + [((2, 512, ROWS), jnp.bfloat16)],
            at,
            row_ids,
            head_orders,
            input_orders,
        )
        mine, line, table, at, head_mine, head_other, placed = lax.optimization_barrier(
            (mine, line, tied_table, at, head_mine, head_other, placed)
        )
        table = hold(table)
    with jax.named_scope("hidden_core"):
        other = other_core(mine)
    with jax.named_scope("cotangent_y"):
        own = [line] + [from_y(line, offset) for offset in (1, 2, 3)]
    with jax.named_scope("logits"):
        logits = [
            sum(
                lax.dot_general(
                    rows[i], half, (((1,), (1,)), ((), ())), preferred_element_type=jnp.float32
                )
                for i, half in enumerate((table[:, :HALF], table[:, HALF:]))
            )
            for rows in (mine, other)
        ]
    with jax.named_scope("stats"):
        (stats,) = small_call(stats_kernel, "stats", [((16, 4, CORE_ROWS), jnp.float32)], at, *logits)
        stats = exchange(stats, "z", "core")
        (stats,) = small_call(merge_kernel, "merge", [((16, 4, CORE_ROWS), jnp.float32)], stats)
        stats, own = lax.optimization_barrier((stats, own))
        far = [other_core(piece) for piece in own]
        stats = exchange(stats, "yl", "yh", "x")
    with jax.named_scope("coefficient"):
        coefficient = small_call(
            coefficient_kernel,
            "coefficient",
            [((CORE_ROWS, 512), jnp.bfloat16)] * 2,
            at,
            *logits,
            stats,
            head_mine,
            head_other,
        )
        *coefficient, own, far = lax.optimization_barrier((*coefficient, own, far))
    with jax.named_scope("hidden_grad"):
        halves = (table[:, :HALF], table[:, HALF:])
        product = lambda rows, half: jnp.dot(rows, half, preferred_element_type=jnp.float32)
        theirs = [other_core(product(coefficient[1], half).astype(jnp.bfloat16)) for half in halves]
        ours = lax.optimization_barrier([product(coefficient[0], half) for half in halves])
        chip = jnp.stack([(a + b).astype(jnp.bfloat16) for a, b in zip(ours, theirs)])
    with jax.named_scope("hidden_grad"):
        (turned,) = small_call(
            turn_kernel,
            "turn",
            [],
            *coefficient,
            far_outs=[((512, ROWS), jnp.bfloat16)],
            scratch=[pltpu.VMEM((512, ROWS), jnp.bfloat16), pltpu.SemaphoreType.DMA],
        )
        chip, turned = lax.optimization_barrier((chip, turned))
        plane = exchange(chip.reshape(16, 24, HALF), "yl", "yh", "x")
        plane, turned, own, far = lax.optimization_barrier((plane, turned, own, far))
        (plane,) = small_call(plane_kernel, "plane_sum", [((16, 2, 3 * HALF // 2), jnp.bfloat16)], plane)
        last = exchange(plane, "yl", "z")
        table_grad = table_grad_call(at, turned, placed, mine, other, own, far)
        last, table_grad = lax.optimization_barrier((last, table_grad))
        (hidden_grad,) = small_call(last_kernel, "last_sum", [((3, D), jnp.bfloat16)], last)
    return (table_grad, hidden_grad)


def solution(mesh):
    placed = (P("section", ("dp", "vocab"), None), P(("section", "dp", "vocab"), None), P())
    return jax.shard_map(
        shards,
        mesh=mesh,
        in_specs=placed,
        out_specs=(P(("section", "dp", "vocab"), None), P(("dp", "vocab"), None)),
        check_vma=False,
    )
```

```python
import math

import jax
import jax.numpy as jnp
from jax import lax
from jax.experimental import pallas as pl
from jax.experimental.pallas import tpu as pltpu
from jax.sharding import PartitionSpec as P

D = 4608
HALF = D // 2
ROWS = 384
CORE_ROWS = 192
CHUNK = 768
PER_HALF = HALF // CHUNK
AXES = ("section", "dp", "vocab")
SIZES = {"yl": 2, "yh": 2, "core": 2, "z": 8, "x": 4}
FACTOR = float(jnp.bfloat16(math.sqrt(D)))


def place(device):
    vocab, dp, section = device % 32, device // 32 % 4, device // 128
    return {"yl": section, "yh": dp // 2, "core": dp % 2, "z": vocab // 4, "x": vocab % 4}


def device_at(at):
    return (at["yl"] * 4 + at["yh"] * 2 + at["core"]) * 32 + at["z"] * 4 + at["x"]


def groups(*axes):
    found = {}
    for device in range(256):
        at = place(device)
        key = tuple(at[a] for a in SIZES if a not in axes)
        found.setdefault(key, []).append((tuple(at[a] for a in axes), device))
    return [[device for _, device in sorted(members)] for members in found.values()]


def exchange(blocks, *axes):
    return lax.all_to_all(blocks, AXES, 0, 0, axis_index_groups=groups(*axes), tiled=True)


def other_core(array):
    pairs = [pair for a, b in groups("core") for pair in ((a, b), (b, a))]
    return lax.ppermute(array, AXES, pairs)


def from_x(array, offset):
    pairs = []
    for device in range(256):
        at = place(device)
        pairs.append((device_at(dict(at, x=(at["x"] + offset) % 4)), device))
    return lax.ppermute(array, AXES, pairs)


def from_y(array, offset):
    pairs = []
    for device in range(256):
        at = place(device)
        y = (at["yh"] * 2 + at["yl"] + offset) % 4
        pairs.append((device_at(dict(at, yh=y // 2, yl=y % 2)), device))
    return lax.ppermute(array, AXES, pairs)


def natural_row(yh, core, z, x, j):
    return ((yh * 2 + core) * 32 + z * 4 + x) * 3 + j


def params(**more):
    return pltpu.CompilerParams(vmem_limit_bytes=14 * 2**20, **more)


def pick(condition, a, b):
    return jnp.where(condition, a, b)


def in_hbm(array):
    return pltpu.with_memory_space_constraint(array, pltpu.MemorySpace.HBM)


def hold_kernel(source, held, arrived):
    copies = []
    for i in range(8):
        rows = slice(64 * i, 64 * i + 64)
        copies.append(pltpu.make_async_copy(source.at[rows, :], held.at[rows, :], arrived.at[i]))
        copies[-1].start()
    for copy in copies:
        copy.wait()


def hold(array):
    return pl.pallas_call(
        hold_kernel,
        in_specs=[pl.BlockSpec(memory_space=pltpu.MemorySpace.HBM)],
        out_specs=pl.BlockSpec(memory_space=pltpu.VMEM),
        out_shape=pltpu.VMEM(array.shape, array.dtype),
        scratch_shapes=[pltpu.SemaphoreType.DMA((8,))],
        compiler_params=params(),
        name="hold",
    )(in_hbm(array))


def ids_onehot(ids, first, order, value):
    column = first + lax.broadcasted_iota(jnp.int32, (512, ROWS), 0)
    plain = jnp.where(column == ids, jnp.float32(value), jnp.float32(0)).astype(jnp.bfloat16)
    natural = lax.broadcasted_iota(jnp.int32, (ROWS, order.shape[1]), 0)
    move = jnp.where(natural == order, jnp.float32(1), jnp.float32(0)).astype(jnp.bfloat16)
    return jnp.dot(plain, move, preferred_element_type=jnp.float32)


HBM = pltpu.MemorySpace.HBM
SCALARS = pl.BlockSpec(memory_space=pltpu.SMEM)
BLOCK = pl.BlockSpec(memory_space=pltpu.VMEM)


def fold(rows):
    top = jnp.concatenate([rows[0:1], rows[1:2, : HALF // 2]], axis=1)
    return jnp.concatenate([top, jnp.concatenate([rows[1:2, HALF // 2 :], rows[2:3]], axis=1)], axis=0)


def unfold(pair):
    middle = jnp.concatenate([pair[0:1, HALF:], pair[1:2, : HALF // 2]], axis=1)
    return jnp.concatenate([pair[0:1, :HALF], middle, pair[1:2, HALF // 2 :]], axis=0)


def first_kernel(source, out, rows, arrived):
    copy = pltpu.make_async_copy(source, rows, arrived)
    copy.start()
    copy.wait()
    for i in range(2):
        half = fold(rows[0, :, i * HALF : (i + 1) * HALF].astype(jnp.float32)).astype(jnp.bfloat16)
        for k in range(8):
            out[8 * i + k] = half


def last_kernel(blocks, out):
    for i in range(2):
        total = blocks[8 * i].astype(jnp.float32)
        for k in range(1, 8):
            total += blocks[8 * i + k].astype(jnp.float32)
        out[:, i * HALF : (i + 1) * HALF] = unfold(total).astype(jnp.bfloat16)


def rows_kernel(got, cotangent, blocks, hidden, sent):
    merge = lambda begin: jnp.concatenate([unfold(got[begin + k].astype(jnp.float32)) for k in range(8)], axis=0)
    hidden[...] = merge(8).astype(jnp.bfloat16)
    copies = []
    for i in range(16):
        copies.append(pltpu.make_async_copy(hidden, blocks.at[i], sent.at[i]))
        copies[-1].start()
    cotangent[...] = merge(0).astype(jnp.bfloat16)
    for copy in copies:
        copy.wait()


def stats_kernel(at, mine, other, out):
    rows = []
    for logits in (mine, other):
        turned = logits[...].T
        high = jnp.max(turned, axis=0, keepdims=True)
        rows.append((high, jnp.sum(jnp.exp(turned - high), axis=0, keepdims=True)))
    first = at[0] == 0
    both = [pick(first, rows[i][k], rows[1 - i][k]) for k in range(2) for i in range(2)]
    out[...] = jnp.broadcast_to(jnp.concatenate(both, axis=0)[None], out.shape)


def merged(parts):
    high = jnp.max(parts[:, 0:2, :], axis=0)
    total = jnp.sum(parts[:, 2:4, :] * jnp.exp(parts[:, 0:2, :] - high), axis=0)
    return high, total


def merge_kernel(parts, out):
    out[...] = jnp.broadcast_to(jnp.concatenate(merged(parts[...]), axis=0)[None], out.shape)


def coefficient_kernel(at, mine, other, parts, head_mine, head_other, out_mine, out_other):
    high, total = merged(parts[...])
    scale = 1.0 / total
    first = at[0] == 0
    sides = ((mine, head_mine, out_mine), (other, head_other, out_other))
    for i, (logits, onehot, out) in enumerate(sides):
        top = pick(first, high[i : i + 1], high[1 - i : 2 - i])
        factor = pick(first, scale[i : i + 1], scale[1 - i : 2 - i])
        values = jnp.exp(logits[...].T - top) * factor - onehot[...].astype(jnp.float32)
        out[...] = values.T.astype(jnp.bfloat16)


def turn_kernel(mine, other, turned, kept, sent):
    kept[...] = jnp.concatenate([mine[...], other[...]], axis=0).T
    copy = pltpu.make_async_copy(kept, turned, sent)
    copy.start()
    copy.wait()


def onehots_kernel(at, ids, head_orders, input_orders, head_mine, head_other, placed):
    for i, out in enumerate((head_mine, head_other)):
        out[...] = ids_onehot(ids[1:2, :], at[2], head_orders[i : i + 1, :], 1.0).astype(jnp.bfloat16)
    for i in range(2):
        placed[i] = ids_onehot(ids[0:1, :], at[2], input_orders[i : i + 1, :], FACTOR).astype(jnp.bfloat16)


def plane_kernel(blocks, out):
    total = blocks[0].astype(jnp.float32)
    for i in range(1, blocks.shape[0]):
        total += blocks[i].astype(jnp.float32)
    for k in range(8):
        rows = fold(total[3 * k : 3 * k + 3]).astype(jnp.bfloat16)
        out[k] = rows
        out[8 + k] = rows


def small_call(kernel, name, outs, *args, far_outs=(), scratch=()):
    return pl.pallas_call(
        kernel,
        in_specs=[SCALARS if a.ndim == 1 else BLOCK for a in args],
        out_specs=[BLOCK] * len(outs) + [pl.BlockSpec(memory_space=HBM)] * len(far_outs),
        out_shape=[jax.ShapeDtypeStruct(*out) for out in outs] + [HBM(*out) for out in far_outs],
        scratch_shapes=scratch,
        compiler_params=params(),
        name=name,
    )(*args)


def table_grad_kernel(at, turned, placed, mine, other, *refs):
    own, far, (out, left, right, done, left_sem, right_sem, done_sem) = refs[:4], refs[4:8], refs[8:]
    lefts = []
    for part in range(2):
        for i, source in enumerate((turned, placed.at[part])):
            target = left.at[part, :, i * ROWS : (i + 1) * ROWS]
            lefts.append(pltpu.make_async_copy(source, target, left_sem.at[part, i]))

    def load(step):
        part, slot = step // PER_HALF, step % 2
        side = lax.bitwise_xor(at[1], part)
        columns = pl.ds(step % PER_HALF * CHUNK, CHUNK)
        sources = [mine.at[side, :, columns], other.at[side, :, columns]]
        sources += [rows[i].at[:, columns] for rows in (own, far) for i in (part, part + 2)]
        copies, begin = [], 0
        for i, source in enumerate(sources):
            rows = CORE_ROWS if i < 2 else 96
            copies.append(
                pltpu.make_async_copy(source, right.at[slot, begin : begin + rows, :], right_sem.at[slot, i])
            )
            begin += rows
        return copies

    def store(step):
        part, slot = step // PER_HALF, step % 2
        side = lax.bitwise_xor(at[1], part)
        begin = pl.multiple_of((side * PER_HALF + step % PER_HALF) * CHUNK, CHUNK)
        return pltpu.make_async_copy(done.at[slot], out.at[:, pl.ds(begin, CHUNK)], done_sem.at[slot])

    steps = 2 * PER_HALF
    loads, stores = [load(step) for step in range(steps)], [store(step) for step in range(steps)]
    for copy in lefts[:2] + loads[0] + lefts[2:]:
        copy.start()
    for step in range(steps):
        if step + 1 < steps:
            for copy in loads[step + 1]:
                copy.start()
        part, slot = step // PER_HALF, step % 2
        if step % PER_HALF == 0:
            for copy in lefts[2 * part : 2 * part + 2]:
                copy.wait()
        for copy in loads[step]:
            copy.wait()
        if step >= 2:
            stores[step - 2].wait()
        total = jnp.dot(left[part], right[slot], preferred_element_type=jnp.float32)
        done[slot] = total.astype(jnp.bfloat16)
        stores[step].start()
    for copy in stores[-2:]:
        copy.wait()


def table_grad_call(at, turned, placed, mine, other, own, far):
    arrays = [in_hbm(a) for a in (turned, placed, mine, other, *own, *far)]
    return pl.pallas_call(
        table_grad_kernel,
        in_specs=[SCALARS] + [pl.BlockSpec(memory_space=HBM)] * len(arrays),
        out_specs=pl.BlockSpec(memory_space=HBM),
        out_shape=jax.ShapeDtypeStruct((512, D), jnp.bfloat16),
        scratch_shapes=[
            pltpu.VMEM((2, 512, 2 * ROWS), jnp.bfloat16),
            pltpu.VMEM((2, 2 * ROWS, CHUNK), jnp.bfloat16),
            pltpu.VMEM((2, 512, CHUNK), jnp.bfloat16),
            pltpu.SemaphoreType.DMA((2, 2)),
            pltpu.SemaphoreType.DMA((2, 6)),
            pltpu.SemaphoreType.DMA((2,)),
        ],
        compiler_params=params(),
        cost_estimate=pl.CostEstimate(flops=4 * ROWS * 512 * D, bytes_accessed=13_000_000, transcendentals=0),
        name="table_grad",
    )(at, *arrays)


def shards(stacked_rows, tied_table, row_ids):
    section, dp, vocab = (lax.axis_index(a) for a in AXES)
    core, yh, x = dp % 2, dp // 2, vocab % 4
    first_column = ((section * 4 + dp) * 32 + vocab) * tied_table.shape[0]
    at = jnp.stack([core, section, first_column]).astype(jnp.int32)

    with jax.named_scope("orders"):
        i = lax.iota(jnp.int32, ROWS)
        c, yy, xx, z, j = i // 192, i // 96 % 2, i // 24 % 4, i // 3 % 8, i % 3
        moved_x = (x + xx) % 4
        y_of = lambda part: (yh * 2 + section + 2 * yy + part) % 4
        head_orders = natural_row(yy, lax.bitwise_xor(core, c), z, xx, j).reshape(2, CORE_ROWS)
        input_orders = jnp.stack(
            [natural_row(y_of(part) // 2, lax.bitwise_xor(core, c), z, moved_x, j) for part in range(2)]
        )

    with jax.named_scope("rows_lz"):
        blocks = pl.pallas_call(
            first_kernel,
            in_specs=[pl.BlockSpec(memory_space=HBM)],
            out_specs=BLOCK,
            out_shape=jax.ShapeDtypeStruct((16, 2, 3 * HALF // 2), jnp.bfloat16),
            scratch_shapes=[pltpu.VMEM((1, 3, D), jnp.bfloat16), pltpu.SemaphoreType.DMA],
            compiler_params=params(),
            name="first_blocks",
        )(in_hbm(stacked_rows))
        cotangent, blocks = small_call(
            rows_kernel,
            "rows",
            [((24, HALF), jnp.bfloat16)],
            exchange(blocks, "yl", "z"),
            far_outs=[((16, 24, HALF), jnp.bfloat16)],
            scratch=[pltpu.VMEM((24, HALF), jnp.bfloat16), pltpu.SemaphoreType.DMA((16,))],
        )
    with jax.named_scope("cotangent_x"):
        line = [cotangent] + [from_x(cotangent, offset) for offset in (1, 2, 3)]
    with jax.named_scope("hidden_xy"):
        mine = exchange(blocks, "yl", "yh", "x").reshape(2, CORE_ROWS, HALF)
        line = jnp.concatenate(line, axis=0)
        head_mine, head_other, placed = small_call(
            onehots_kernel,
            "onehots",
            [((512, CORE_ROWS), jnp.bfloat16)] * 2 + [((2, 512, ROWS), jnp.bfloat16)],
            at,
            row_ids,
            head_orders,
            input_orders,
        )
        mine, line, table, at, head_mine, head_other, placed = lax.optimization_barrier(
            (mine, line, tied_table, at, head_mine, head_other, placed)
        )
        table = hold(table)
    with jax.named_scope("hidden_core"):
        other = other_core(mine)
    with jax.named_scope("cotangent_y"):
        own = [line] + [from_y(line, offset) for offset in (1, 2, 3)]
    with jax.named_scope("logits"):
        logits = [
            sum(
                lax.dot_general(
                    rows[i], half, (((1,), (1,)), ((), ())), preferred_element_type=jnp.float32
                )
                for i, half in enumerate((table[:, :HALF], table[:, HALF:]))
            )
            for rows in (mine, other)
        ]
    with jax.named_scope("stats"):
        (stats,) = small_call(stats_kernel, "stats", [((16, 4, CORE_ROWS), jnp.float32)], at, *logits)
        stats = exchange(stats, "z", "core")
        (stats,) = small_call(merge_kernel, "merge", [((16, 4, CORE_ROWS), jnp.float32)], stats)
        stats, own = lax.optimization_barrier((stats, own))
        far = [other_core(piece) for piece in own]
        stats = exchange(stats, "yl", "yh", "x")
    with jax.named_scope("coefficient"):
        coefficient = small_call(
            coefficient_kernel,
            "coefficient",
            [((CORE_ROWS, 512), jnp.bfloat16)] * 2,
            at,
            *logits,
            stats,
            head_mine,
            head_other,
        )
        *coefficient, own, far = lax.optimization_barrier((*coefficient, own, far))
    with jax.named_scope("hidden_grad"):
        halves = (table[:, :HALF], table[:, HALF:])
        product = lambda rows, half: jnp.dot(rows, half, preferred_element_type=jnp.float32)
        theirs = [other_core(product(coefficient[1], half).astype(jnp.bfloat16)) for half in halves]
        ours = lax.optimization_barrier([product(coefficient[0], half) for half in halves])
        chip = jnp.stack([(a + b).astype(jnp.bfloat16) for a, b in zip(ours, theirs)])
    with jax.named_scope("hidden_grad"):
        (turned,) = small_call(
            turn_kernel,
            "turn",
            [],
            *coefficient,
            far_outs=[((512, ROWS), jnp.bfloat16)],
            scratch=[pltpu.VMEM((512, ROWS), jnp.bfloat16), pltpu.SemaphoreType.DMA],
        )
        chip, turned = lax.optimization_barrier((chip, turned))
        plane = exchange(chip.reshape(16, 24, HALF), "yl", "yh", "x")
        plane, turned, own, far = lax.optimization_barrier((plane, turned, own, far))
        (plane,) = small_call(plane_kernel, "plane_sum", [((16, 2, 3 * HALF // 2), jnp.bfloat16)], plane)
        last = exchange(plane, "yl", "z")
        table_grad = table_grad_call(at, turned, placed, mine, other, own, far)
        last, table_grad = lax.optimization_barrier((last, table_grad))
        (hidden_grad,) = small_call(last_kernel, "last_sum", [((3, D), jnp.bfloat16)], last)
    return (table_grad, hidden_grad)


def solution(mesh):
    placed = (P("section", ("dp", "vocab"), None), P(("section", "dp", "vocab"), None), P())
    return jax.shard_map(
        shards,
        mesh=mesh,
        in_specs=placed,
        out_specs=(P(("section", "dp", "vocab"), None), P(("dp", "vocab"), None)),
        check_vma=False,
    )
```
